32 devices in a mesh: row: 4 (over y, x), col: 4 (over z), layer: 2 (over core).
Axes of the slice: x: 2, y: 2, z: 4, core: 2. Of those that a mesh axis runs over, the one named last changes fastest.
Arguments:
- density: bfloat16 [1024, 1024], P('row', 'col'), may hold values from -0.25 to 0.25
- panel: bfloat16 [1024, 8192], P('row', 'col'), may hold values from -6 to 6
- pattern: int32 [8, 8], P('row', 'col'), may hold values 0 or 1
Outputs:
- purified: bfloat16 [1024, 8192], P('row', ('col', 'layer'))
The draws below stay inside these ranges and needn't reach their ends.
All inputs are finite; a program needn't handle non-finite values. No bound on the sum of `pattern` on one device may be relied on, other than what follows from the above.
Results may differ from the reference program's by a relative error of at most 0.0034.
Values may be sent and summed in bfloat16 or wider, within the bound.
A program may use at most 64 MiB of HBM per device.

```python
import jax
import jax.numpy as jnp

BS = 128
NB = 8
K = 1024
PW = 8192


def with_ends(drawn, key, smallest, high):
    index_at = [jax.random.randint(jax.random.fold_in(key, axis), (), 0, length) for axis, length in enumerate(drawn.shape)]
    longest = drawn.shape.index(max(drawn.shape))
    neighbour = index_at[:longest] + [(index_at[longest] + 1) % drawn.shape[longest]] + index_at[longest + 1:]
    return drawn.at[tuple(index_at)].set(smallest).at[tuple(neighbour)].set(high)


def levels(stream_key, dims, pieces, smallest, top_value):
    loudness, own = 1.0, jax.random.fold_in(stream_key, 6)
    for axis_at, shards_of in pieces:
        draws = jnp.exp(jax.random.uniform(jax.random.fold_in(own, axis_at), (shards_of,), jnp.float32, smallest / len(pieces), top_value / len(pieces)))
        loudness = loudness * jnp.repeat(draws, dims[axis_at] // shards_of).reshape([-1 if axis == axis_at else 1 for axis in range(len(dims))])
    return loudness


def scatter_about(own_key, extent, deviation, most, shards=(), kind=jnp.bfloat16):
    result = jax.random.normal(own_key, extent, jnp.float32) * deviation
    if len(shards) > 0:
        result = levels(own_key, extent, shards, -0.22, 0.18) * result
    return jnp.clip(result, min=-most, max=most).astype(kind)


def setup_inputs(seed: int = 0) -> dict:
    key_of = jax.random.split(jax.random.key(seed), 4)
    density = scatter_about(key_of[0], (K, K), (K // 2) ** -0.5, 0.25, ((0, 4), (1, 4)))
    panel = scatter_about(key_of[1], (K, PW), 1.0, 6.0, ((0, 4), (1, 4)))
    pattern = with_ends((jax.random.randint(key_of[2], (NB, NB), 0, 2) < 1).astype(jnp.int32), jax.random.fold_in(key_of[2], 1), 0, 1)
    return dict(density=density, panel=panel, pattern=pattern)


def reference(density, panel, pattern):
    expanded = jnp.repeat(jnp.repeat(pattern, BS, axis=0), BS, axis=1).astype(jnp.bfloat16)
    filtered = density * expanded
    square = jnp.dot(filtered, panel, preferred_element_type=jnp.float32)
    square_low = square.astype(jnp.bfloat16)
    cubic = jnp.dot(filtered, square_low, preferred_element_type=jnp.float32)
    return (3.0 * square - 2.0 * cubic).astype(jnp.bfloat16)
```

```python
import functools

import jax
import jax.numpy as jnp
from jax import lax
from jax.experimental import pallas as pl
from jax.experimental.pallas import tpu as pltpu
from jax.sharding import PartitionSpec as P

BS = 128
PIECES = 4
MESH = pl.DeviceIdType.MESH


def kernel(
    sizes, density_ref, panel_ref, pattern_ref, out_ref,
    tile, fcol, frow, grow, p, acc,
    load_sem, fc_s, fc_r, fr_s, fr_r, fs_s, fs_r, gr_s, gr_r, gs_s, gs_r,
    px_s, px_r, py_s, py_r, fx_s, fx_r, fy_s, fy_r,
):
    R, A, C = sizes
    B = R // A
    tr, ti = density_ref.shape
    half = ti // 2
    W = p.shape[2]
    wq = W // PIECES
    r = lax.axis_index("row")
    c = lax.axis_index("col")
    l = lax.axis_index("layer")
    x = lax.rem(r, A)
    y = r // A
    sib = 1 - l

    def rem_copy(ref, ssem, rsem, dev):
        return pltpu.make_async_remote_copy(
            src_ref=ref, dst_ref=ref, send_sem=ssem, recv_sem=rsem,
            device_id=dev, device_id_type=MESH,
        )

    barrier = pltpu.get_barrier_semaphore()
    for d in range(1, R):
        pl.semaphore_signal(barrier, inc=1, device_id={"row": lax.rem(r + d, R)}, device_id_type=MESH)
    for d in range(1, C):
        pl.semaphore_signal(barrier, inc=1, device_id={"col": lax.rem(c + d, C)}, device_id_type=MESH)
    pl.semaphore_signal(barrier, inc=1, device_id={"layer": sib}, device_id_type=MESH)

    load_tile = pltpu.make_async_copy(density_ref, tile, load_sem.at[0])
    load_tile.start()
    own_cols = pl.ds(pl.multiple_of(l * W, W), W)
    load_panel = pltpu.make_async_copy(panel_ref.at[:, own_cols], p.at[r], load_sem.at[1])
    load_panel.start()
    load_tile.wait()

    for a in range(tr // BS):
        for b in range(ti // BS):
            keep = pattern_ref[a, b].astype(jnp.float32)
            block = tile[a * BS:(a + 1) * BS, b * BS:(b + 1) * BS].astype(jnp.float32) * keep
            at = pl.ds(pl.multiple_of(c * ti + b * BS, BS), BS)
            frow[a * BS:(a + 1) * BS, at] = block.astype(jnp.bfloat16)
    def cols_of(col, layer):
        return pl.ds(pl.multiple_of(col * ti + layer * half, half), half)
    def rows_of(row):
        return pl.ds(pl.multiple_of(row * tr, tr), tr)
    fcol[rows_of(r), :] = frow[:, cols_of(c, l)]

    pl.semaphore_wait(barrier, R - 1 + C - 1 + 1)

    sends = []

    def send(ref, ssem, rsem, dev):
        copy = rem_copy(ref, ssem, rsem, dev)
        copy.start()
        sends.append(copy)

    def arrived(ref, ssem, rsem, dev):
        rem_copy(ref, ssem, rsem, dev).wait_recv()

    for d in range(1, R):
        send(fcol.at[rows_of(r), :], fc_s.at[d], fc_r.at[d], {"row": lax.rem(r + d, R)})
    for d in range(1, C):
        send(frow.at[:, cols_of(c, l)], fr_s.at[d], fr_r.at[d], {"col": lax.rem(c + d, C)})
    load_panel.wait()
    first, second = range(PIECES // 2), range(PIECES // 2, PIECES)

    def piece(row, q):
        return p.at[row, :, q * wq:(q + 1) * wq]

    def x_peer(d):
        return y * A + lax.rem(x + d, A)

    def y_peer(d):
        return lax.rem(y + d, B) * A + x

    x_order = list(second) + list(first)
    y_order = list(first) + list(second)
    for qx, qy in zip(x_order, y_order):
        for d in range(1, A):
            send(piece(r, qx), px_s.at[d, qx], px_r.at[d, qx], {"row": x_peer(d)})
        for d in range(1, B):
            send(piece(r, qy), py_s.at[d, qy], py_r.at[d, qy], {"row": y_peer(d)})

    for d in range(1, C):
        from_c = lax.rem(c - d + C, C)
        ref = frow.at[:, cols_of(from_c, l)]
        arrived(ref, fr_s.at[d], fr_r.at[d], {"col": from_c})
        send(ref, fs_s.at[d], fs_r.at[d], {"layer": sib})
    for d in range(1, C):
        from_c = lax.rem(c - d + C, C)
        arrived(frow.at[:, cols_of(from_c, sib)], fs_s.at[d], fs_r.at[d], {"layer": sib})
    for d in range(1, R):
        from_r = lax.rem(r - d + R, R)
        arrived(fcol.at[rows_of(from_r), :], fc_s.at[d], fc_r.at[d], {"row": from_r})

    grow[:, cols_of(c, l)] = jnp.dot(
        frow[...], fcol[...], preferred_element_type=jnp.float32
    ).astype(jnp.bfloat16)
    for d in range(1, C):
        send(grow.at[:, cols_of(c, l)], gr_s.at[d], gr_r.at[d], {"col": lax.rem(c + d, C)})
    send(grow.at[:, cols_of(c, l)], gs_s.at[0], gs_r.at[0], {"layer": sib})

    for qf, qs in zip(first, second):
        for dy in range(1, B):
            row = lax.rem(y - dy + B, B) * A + x
            arrived(piece(row, qf), py_s.at[dy, qf], py_r.at[dy, qf], {"row": row})
            for dx in range(1, A):
                send(piece(row, qf), fx_s.at[dy, dx, qf], fx_r.at[dy, dx, qf], {"row": x_peer(dx)})
        for dx in range(1, A):
            row = y * A + lax.rem(x - dx + A, A)
            arrived(piece(row, qs), px_s.at[dx, qs], px_r.at[dx, qs], {"row": row})
            for dy in range(1, B):
                send(piece(row, qs), fy_s.at[dy, dx, qs], fy_r.at[dy, dx, qs], {"row": y_peer(dy)})

    for d in range(1, C):
        from_c = lax.rem(c - d + C, C)
        ref = grow.at[:, cols_of(from_c, l)]
        arrived(ref, gr_s.at[d], gr_r.at[d], {"col": from_c})
        send(ref, gs_s.at[d], gs_r.at[d], {"layer": sib})
    for d in range(C):
        from_c = lax.rem(c - d + C, C)
        arrived(grow.at[:, cols_of(from_c, sib)], gs_s.at[d], gs_r.at[d], {"layer": sib})

    def term(row, q):
        at = pl.ds(pl.multiple_of(row * tr, tr), tr)
        right = p[row, :, q * wq:(q + 1) * wq]
        by_f = jnp.dot(frow[:, at], right, preferred_element_type=jnp.float32)
        by_g = jnp.dot(grow[:, at], right, preferred_element_type=jnp.float32)
        return 3.0 * by_f - 2.0 * by_g

    def part(q):
        return slice(q * wq, (q + 1) * wq)

    for q in range(PIECES):
        acc[:, part(q)] = term(r, q)
    for dx in range(1, A):
        row = y * A + lax.rem(x - dx + A, A)
        for q in x_order:
            if q in first:
                arrived(piece(row, q), px_s.at[dx, q], px_r.at[dx, q], {"row": row})
            acc[:, part(q)] += term(row, q)
    for dy in range(1, B):
        row = lax.rem(y - dy + B, B) * A + x
        for q in y_order:
            if q in second:
                arrived(piece(row, q), py_s.at[dy, q], py_r.at[dy, q], {"row": row})
            acc[:, part(q)] += term(row, q)
    for qf, qs in zip(first, second):
        for q, s_sem, r_sem in ((qf, fx_s, fx_r), (qs, fy_s, fy_r)):
            for dy in range(1, B):
                for dx in range(1, A):
                    row = lax.rem(y - dy + B, B) * A + lax.rem(x - dx + A, A)
                    arrived(piece(row, q), s_sem.at[dy, dx, q], r_sem.at[dy, dx, q], {"row": row})
            total = acc[:, part(q)]
            for dy in range(1, B):
                for dx in range(1, A):
                    row = lax.rem(y - dy + B, B) * A + lax.rem(x - dx + A, A)
                    total = total + term(row, q)
            out_ref[:, part(q)] = total.astype(jnp.bfloat16)

    for copy in sends:
        copy.wait_send()


def shards(R, C, L, density, panel, pattern):
    A = 1
    while A * A < R:
        A *= 2
    B = R // A
    tr, ti = density.shape
    half = ti // L
    W = panel.shape[1] // L
    K = tr * R
    dma = pltpu.SemaphoreType.DMA
    any_spec = pl.BlockSpec(memory_space=pl.ANY)
    bf16 = jnp.bfloat16
    return pl.pallas_call(
        functools.partial(kernel, (R, A, C)),
        out_shape=jax.ShapeDtypeStruct((tr, W), bf16),
        in_specs=[any_spec, any_spec, pl.BlockSpec(memory_space=pltpu.SMEM)],
        out_specs=pl.BlockSpec(memory_space=pltpu.VMEM),
        scratch_shapes=[
            pltpu.VMEM((tr, ti), bf16),
            pltpu.VMEM((K, half), bf16),
            pltpu.VMEM((tr, K), bf16),
            pltpu.VMEM((tr, K), bf16),
            pltpu.VMEM((R, tr, W), bf16),
            pltpu.VMEM((tr, W), jnp.float32),
            dma((2,)),
            dma((R,)), dma((R,)),
            dma((C,)), dma((C,)), dma((C,)), dma((C,)),
            dma((C,)), dma((C,)), dma((C,)), dma((C,)),
            dma((A, PIECES)), dma((A, PIECES)),
            dma((B, PIECES)), dma((B, PIECES)),
            dma((B, A, PIECES)), dma((B, A, PIECES)),
            dma((B, A, PIECES)), dma((B, A, PIECES)),
        ],
        compiler_params=pltpu.CompilerParams(
            collective_id=0, has_side_effects=True, vmem_limit_bytes=56 * 1024 * 1024
        ),
    )(density, panel, pattern)


def solution(mesh):
    R, C, L = mesh.shape["row"], mesh.shape["col"], mesh.shape["layer"]
    in_specs = (P("row", "col"), P("row", "col"), P("row", "col"))
    out_specs = P("row", ("col", "layer"))
    return jax.shard_map(
        functools.partial(shards, R, C, L),
        mesh=mesh, in_specs=in_specs, out_specs=out_specs, check_vma=False,
    )
```

```python
import functools

import jax
import jax.numpy as jnp
from jax import lax
from jax.experimental import pallas as pl
from jax.experimental.pallas import tpu as pltpu
from jax.sharding import PartitionSpec as P

BS = 128
PIECES = 4
MESH = pl.DeviceIdType.MESH


def kernel(
    sizes, density_ref, panel_ref, pattern_hbm, out_ref,
    pattern_ref, tile, fcol, frow, grow, p, acc,
    load_sem, fc_s, fc_r, fr_s, fr_r, fs_s, fs_r, gr_s, gr_r, gs_s, gs_r,
    px_s, px_r, py_s, py_r, fx_s, fx_r, fy_s, fy_r,
):
    R, A, C = sizes
    B = R // A
    tr, ti = density_ref.shape
    half = ti // 2
    W = p.shape[2]
    wq = W // PIECES
    r = lax.axis_index("row")
    c = lax.axis_index("col")
    l = lax.axis_index("layer")
    x = lax.rem(r, A)
    y = r // A
    sib = 1 - l

    def rem_copy(ref, ssem, rsem, dev):
        return pltpu.make_async_remote_copy(
            src_ref=ref, dst_ref=ref, send_sem=ssem, recv_sem=rsem,
            device_id=dev, device_id_type=MESH,
        )

    barrier = pltpu.get_barrier_semaphore()
    for d in range(1, R):
        pl.semaphore_signal(barrier, inc=1, device_id={"row": lax.rem(r + d, R)}, device_id_type=MESH)
    for d in range(1, C):
        pl.semaphore_signal(barrier, inc=1, device_id={"col": lax.rem(c + d, C)}, device_id_type=MESH)
    pl.semaphore_signal(barrier, inc=1, device_id={"layer": sib}, device_id_type=MESH)

    load_pattern = pltpu.make_async_copy(pattern_hbm, pattern_ref, load_sem.at[2])
    load_pattern.start()
    load_tile = pltpu.make_async_copy(density_ref, tile, load_sem.at[0])
    load_tile.start()
    own_cols = pl.ds(pl.multiple_of(l * W, W), W)
    load_panel = pltpu.make_async_copy(panel_ref.at[:, own_cols], p.at[r], load_sem.at[1])
    load_panel.start()
    load_pattern.wait()
    load_tile.wait()

    for a in range(tr // BS):
        for b in range(ti // BS):
            keep = pattern_ref[a, b].astype(jnp.float32)
            block = tile[a * BS:(a + 1) * BS, b * BS:(b + 1) * BS].astype(jnp.float32) * keep
            at = pl.ds(pl.multiple_of(c * ti + b * BS, BS), BS)
            frow[a * BS:(a + 1) * BS, at] = block.astype(jnp.bfloat16)
    def cols_of(col, layer):
        return pl.ds(pl.multiple_of(col * ti + layer * half, half), half)
    def rows_of(row):
        return pl.ds(pl.multiple_of(row * tr, tr), tr)
    fcol[rows_of(r), :] = frow[:, cols_of(c, l)]

    pl.semaphore_wait(barrier, R - 1 + C - 1 + 1)

    sends = []

    def send(ref, ssem, rsem, dev):
        copy = rem_copy(ref, ssem, rsem, dev)
        copy.start()
        sends.append(copy)

    def arrived(ref, ssem, rsem, dev):
        rem_copy(ref, ssem, rsem, dev).wait_recv()

    for d in range(1, R):
        send(fcol.at[rows_of(r), :], fc_s.at[d], fc_r.at[d], {"row": lax.rem(r + d, R)})
    for d in range(1, C):
        send(frow.at[:, cols_of(c, l)], fr_s.at[d], fr_r.at[d], {"col": lax.rem(c + d, C)})
    load_panel.wait()
    first, second = range(PIECES // 2), range(PIECES // 2, PIECES)

    def piece(row, q):
        return p.at[row, :, q * wq:(q + 1) * wq]

    def x_peer(d):
        return y * A + lax.rem(x + d, A)

    def y_peer(d):
        return lax.rem(y + d, B) * A + x

    x_order = list(second) + list(first)
    y_order = list(first) + list(second)
    for qx, qy in zip(x_order, y_order):
        for d in range(1, A):
            send(piece(r, qx), px_s.at[d, qx], px_r.at[d, qx], {"row": x_peer(d)})
        for d in range(1, B):
            send(piece(r, qy), py_s.at[d, qy], py_r.at[d, qy], {"row": y_peer(d)})

    for d in range(1, C):
        from_c = lax.rem(c - d + C, C)
        ref = frow.at[:, cols_of(from_c, l)]
        arrived(ref, fr_s.at[d], fr_r.at[d], {"col": from_c})
        send(ref, fs_s.at[d], fs_r.at[d], {"layer": sib})
    for d in range(1, C):
        from_c = lax.rem(c - d + C, C)
        arrived(frow.at[:, cols_of(from_c, sib)], fs_s.at[d], fs_r.at[d], {"layer": sib})
    for d in range(1, R):
        from_r = lax.rem(r - d + R, R)
        arrived(fcol.at[rows_of(from_r), :], fc_s.at[d], fc_r.at[d], {"row": from_r})

    grow[:, cols_of(c, l)] = jnp.dot(
        frow[...], fcol[...], preferred_element_type=jnp.float32
    ).astype(jnp.bfloat16)
    for d in range(1, C):
        send(grow.at[:, cols_of(c, l)], gr_s.at[d], gr_r.at[d], {"col": lax.rem(c + d, C)})
    send(grow.at[:, cols_of(c, l)], gs_s.at[0], gs_r.at[0], {"layer": sib})

    def part(q):
        return slice(q * wq, (q + 1) * wq)

    def by(left, row, q):
        at = pl.ds(pl.multiple_of(row * tr, tr), tr)
        return jnp.dot(left[:, at], p[row, :, part(q)], preferred_element_type=jnp.float32)

    def term(row, q):
        return 3.0 * by(frow, row, q) - 2.0 * by(grow, row, q)

    for q in range(PIECES):
        acc[:, part(q)] = 3.0 * by(frow, r, q)

    for qf, qs in zip(first, second):
        for dy in range(1, B):
            row = lax.rem(y - dy + B, B) * A + x
            arrived(piece(row, qf), py_s.at[dy, qf], py_r.at[dy, qf], {"row": row})
            for dx in range(1, A):
                send(piece(row, qf), fx_s.at[dy, dx, qf], fx_r.at[dy, dx, qf], {"row": x_peer(dx)})
        for dx in range(1, A):
            row = y * A + lax.rem(x - dx + A, A)
            arrived(piece(row, qs), px_s.at[dx, qs], px_r.at[dx, qs], {"row": row})
            for dy in range(1, B):
                send(piece(row, qs), fy_s.at[dy, dx, qs], fy_r.at[dy, dx, qs], {"row": y_peer(dy)})

    for d in range(1, C):
        from_c = lax.rem(c - d + C, C)
        ref = grow.at[:, cols_of(from_c, l)]
        arrived(ref, gr_s.at[d], gr_r.at[d], {"col": from_c})
        send(ref, gs_s.at[d], gs_r.at[d], {"layer": sib})
    for d in range(C):
        from_c = lax.rem(c - d + C, C)
        arrived(grow.at[:, cols_of(from_c, sib)], gs_s.at[d], gs_r.at[d], {"layer": sib})

    for q in range(PIECES):
        acc[:, part(q)] -= 2.0 * by(grow, r, q)
    for dx in range(1, A):
        row = y * A + lax.rem(x - dx + A, A)
        for q in x_order:
            if q in first:
                arrived(piece(row, q), px_s.at[dx, q], px_r.at[dx, q], {"row": row})
            acc[:, part(q)] += term(row, q)
    for dy in range(1, B):
        row = lax.rem(y - dy + B, B) * A + x
        for q in y_order:
            if q in second:
                arrived(piece(row, q), py_s.at[dy, q], py_r.at[dy, q], {"row": row})
            acc[:, part(q)] += term(row, q)
    for qf, qs in zip(first, second):
        for q, s_sem, r_sem in ((qf, fx_s, fx_r), (qs, fy_s, fy_r)):
            for dy in range(1, B):
                for dx in range(1, A):
                    row = lax.rem(y - dy + B, B) * A + lax.rem(x - dx + A, A)
                    arrived(piece(row, q), s_sem.at[dy, dx, q], r_sem.at[dy, dx, q], {"row": row})
            total = acc[:, part(q)]
            for dy in range(1, B):
                for dx in range(1, A):
                    row = lax.rem(y - dy + B, B) * A + lax.rem(x - dx + A, A)
                    total = total + term(row, q)
            out_ref[:, part(q)] = total.astype(jnp.bfloat16)

    for copy in sends:
        copy.wait_send()


def shards(R, C, L, density, panel, pattern):
    A = 1
    while A * A < R:
        A *= 2
    B = R // A
    tr, ti = density.shape
    half = ti // L
    W = panel.shape[1] // L
    K = tr * R
    dma = pltpu.SemaphoreType.DMA
    any_spec = pl.BlockSpec(memory_space=pl.ANY)
    bf16 = jnp.bfloat16
    return pl.pallas_call(
        functools.partial(kernel, (R, A, C)),
        out_shape=pltpu.VMEM((tr, W), bf16),
        in_specs=[any_spec] * 3,
        out_specs=pl.BlockSpec(memory_space=pltpu.VMEM),
        scratch_shapes=[
            pltpu.SMEM(pattern.shape, jnp.int32),
            pltpu.VMEM((tr, ti), bf16),
            pltpu.VMEM((K, half), bf16),
            pltpu.VMEM((tr, K), bf16),
            pltpu.VMEM((tr, K), bf16),
            pltpu.VMEM((R, tr, W), bf16),
            pltpu.VMEM((tr, W), jnp.float32),
            dma((3,)),
            dma((R,)), dma((R,)),
            dma((C,)), dma((C,)), dma((C,)), dma((C,)),
            dma((C,)), dma((C,)), dma((C,)), dma((C,)),
            dma((A, PIECES)), dma((A, PIECES)),
            dma((B, PIECES)), dma((B, PIECES)),
            dma((B, A, PIECES)), dma((B, A, PIECES)),
            dma((B, A, PIECES)), dma((B, A, PIECES)),
        ],
        compiler_params=pltpu.CompilerParams(
            collective_id=0, has_side_effects=True, vmem_limit_bytes=56 * 1024 * 1024
        ),
    )(density, panel, pattern)


def solution(mesh):
    R, C, L = mesh.shape["row"], mesh.shape["col"], mesh.shape["layer"]
    in_specs = (P("row", "col"), P("row", "col"), P("row", "col"))
    out_specs = P("row", ("col", "layer"))
    return jax.shard_map(
        functools.partial(shards, R, C, L),
        mesh=mesh, in_specs=in_specs, out_specs=out_specs, check_vma=False,
    )
```

```python
import functools

import jax
import jax.numpy as jnp
from jax import lax
from jax.experimental import pallas as pl
from jax.experimental.pallas import tpu as pltpu
from jax.sharding import PartitionSpec as P

BS = 128
PIECES = 4
MESH = pl.DeviceIdType.MESH


def kernel(
    sizes, density_ref, panel_ref, pattern_hbm, out_ref,
    pattern_ref, tile, fcol, frow, grow, p, acc,
    load_sem, cx_s, cx_r, cy_s, cy_r, ex_s, ex_r, ey_s, ey_r, fr_s, fr_r, fs_s, fs_r, gr_s, gr_r, gs_s, gs_r,
    px_s, px_r, py_s, py_r, fx_s, fx_r, fy_s, fy_r,
):
    R, A, C = sizes
    B = R // A
    tr, ti = density_ref.shape
    half = ti // 2
    W = p.shape[2]
    wq = W // PIECES
    r = lax.axis_index("row")
    c = lax.axis_index("col")
    l = lax.axis_index("layer")
    x = lax.rem(r, A)
    y = r // A
    sib = 1 - l

    def rem_copy(ref, ssem, rsem, dev):
        return pltpu.make_async_remote_copy(
            src_ref=ref, dst_ref=ref, send_sem=ssem, recv_sem=rsem,
            device_id=dev, device_id_type=MESH,
        )

    def x_peer(d):
        return y * A + lax.rem(x + d, A)

    def y_peer(d):
        return lax.rem(y + d, B) * A + x

    barrier = pltpu.get_barrier_semaphore()
    for d in range(1, A):
        pl.semaphore_signal(barrier, inc=1, device_id={"row": x_peer(d)}, device_id_type=MESH)
    for d in range(1, B):
        pl.semaphore_signal(barrier, inc=1, device_id={"row": y_peer(d)}, device_id_type=MESH)
    for d in range(1, C):
        pl.semaphore_signal(barrier, inc=1, device_id={"col": lax.rem(c + d, C)}, device_id_type=MESH)
    pl.semaphore_signal(barrier, inc=1, device_id={"layer": sib}, device_id_type=MESH)

    load_pattern = pltpu.make_async_copy(pattern_hbm, pattern_ref, load_sem.at[2])
    load_pattern.start()
    load_tile = pltpu.make_async_copy(density_ref, tile, load_sem.at[0])
    load_tile.start()
    own_cols = pl.ds(pl.multiple_of(l * W, W), W)
    load_panel = pltpu.make_async_copy(panel_ref.at[:, own_cols], p.at[r], load_sem.at[1])
    load_panel.start()
    first, second = range(PIECES // 2), range(PIECES // 2, PIECES)

    def cols_of(col, layer):
        return pl.ds(pl.multiple_of(col * ti + layer * half, half), half)

    def rows_of(row):
        return pl.ds(pl.multiple_of(row * tr, tr), tr)

    def half_rows(row, which):
        return fcol.at[pl.ds(pl.multiple_of(row * tr + which * (tr // 2), tr // 2), tr // 2), :]

    def piece(row, q):
        return p.at[row, :, q * wq:(q + 1) * wq]

    def x_source(d):
        return y * A + lax.rem(x - d + A, A)

    def y_source(d):
        return lax.rem(y - d + B, B) * A + x

    def both_source(dy, dx):
        return lax.rem(y - dy + B, B) * A + lax.rem(x - dx + A, A)

    sends = []

    def send(ref, ssem, rsem, dev, src=None):
        copy = pltpu.make_async_remote_copy(
            src_ref=ref if src is None else src, dst_ref=ref, send_sem=ssem, recv_sem=rsem,
            device_id=dev, device_id_type=MESH,
        )
        copy.start()
        sends.append(copy)

    def arrived(ref, ssem, rsem, dev):
        rem_copy(ref, ssem, rsem, dev).wait_recv()

    x_order = list(second) + list(first)
    y_order = list(first) + list(second)

    def send_own(n, from_hbm=False):
        def src(q):
            at = pl.ds(pl.multiple_of(l * W + q * wq, wq), wq)
            return panel_ref.at[:, at] if from_hbm else None
        qx, qy = x_order[n], y_order[n]
        for d in range(1, A):
            send(piece(r, qx), px_s.at[d, qx], px_r.at[d, qx], {"row": x_peer(d)}, src(qx))
        for d in range(1, B):
            send(piece(r, qy), py_s.at[d, qy], py_r.at[d, qy], {"row": y_peer(d)}, src(qy))

    pl.semaphore_wait(barrier, A - 1 + B - 1 + C - 1 + 1)
    send_own(0, from_hbm=True)

    load_pattern.wait()
    load_tile.wait()
    for a in range(tr // BS):
        for b in range(ti // BS):
            keep = pattern_ref[a, b].astype(jnp.float32)
            block = tile[a * BS:(a + 1) * BS, b * BS:(b + 1) * BS].astype(jnp.float32) * keep
            at = pl.ds(pl.multiple_of(c * ti + b * BS, BS), BS)
            frow[a * BS:(a + 1) * BS, at] = block.astype(jnp.bfloat16)
    for d in range(1, C):
        send(frow.at[:, cols_of(c, l)], fr_s.at[d], fr_r.at[d], {"col": lax.rem(c + d, C)})
    fcol[rows_of(r), :] = frow[:, cols_of(c, l)]
    for d in range(1, A):
        send(fcol.at[rows_of(r), :], cx_s.at[d], cx_r.at[d], {"row": x_peer(d)})
    for d in range(1, B):
        send(fcol.at[rows_of(r), :], cy_s.at[d], cy_r.at[d], {"row": y_peer(d)})
    load_panel.wait()
    send_own(1)

    for dy in range(1, B):
        row = y_source(dy)
        arrived(fcol.at[rows_of(row), :], cy_s.at[dy], cy_r.at[dy], {"row": row})
        for dx in range(1, A):
            send(half_rows(row, 0), ex_s.at[dy, dx], ex_r.at[dy, dx], {"row": x_peer(dx)})
    for dx in range(1, A):
        row = x_source(dx)
        arrived(fcol.at[rows_of(row), :], cx_s.at[dx], cx_r.at[dx], {"row": row})
        for dy in range(1, B):
            send(half_rows(row, 1), ey_s.at[dy, dx], ey_r.at[dy, dx], {"row": y_peer(dy)})
    for n in range(2, PIECES):
        send_own(n)

    for d in range(1, C):
        from_c = lax.rem(c - d + C, C)
        ref = frow.at[:, cols_of(from_c, l)]
        arrived(ref, fr_s.at[d], fr_r.at[d], {"col": from_c})
        send(ref, fs_s.at[d], fs_r.at[d], {"layer": sib})
    for d in range(1, C):
        from_c = lax.rem(c - d + C, C)
        arrived(frow.at[:, cols_of(from_c, sib)], fs_s.at[d], fs_r.at[d], {"layer": sib})
    for dy in range(1, B):
        for dx in range(1, A):
            row = both_source(dy, dx)
            arrived(half_rows(row, 0), ex_s.at[dy, dx], ex_r.at[dy, dx], {"row": row})
            arrived(half_rows(row, 1), ey_s.at[dy, dx], ey_r.at[dy, dx], {"row": row})

    grow[:, cols_of(c, l)] = jnp.dot(
        frow[...], fcol[...], preferred_element_type=jnp.float32
    ).astype(jnp.bfloat16)
    for d in range(1, C):
        send(grow.at[:, cols_of(c, l)], gr_s.at[d], gr_r.at[d], {"col": lax.rem(c + d, C)})
    send(grow.at[:, cols_of(c, l)], gs_s.at[0], gs_r.at[0], {"layer": sib})

    def part(q):
        return slice(q * wq, (q + 1) * wq)

    def by(left, row, q):
        at = pl.ds(pl.multiple_of(row * tr, tr), tr)
        return jnp.dot(left[:, at], p[row, :, part(q)], preferred_element_type=jnp.float32)

    def term(row, q):
        return 3.0 * by(frow, row, q) - 2.0 * by(grow, row, q)

    for q in range(PIECES):
        acc[:, part(q)] = 3.0 * by(frow, r, q)

    early = len(sends)
    for qf, qs in zip(first, second):
        for dy in range(1, B):
            row = y_source(dy)
            arrived(piece(row, qf), py_s.at[dy, qf], py_r.at[dy, qf], {"row": row})
            for dx in range(1, A):
                send(piece(row, qf), fx_s.at[dy, dx, qf], fx_r.at[dy, dx, qf], {"row": x_peer(dx)})
        for dx in range(1, A):
            row = x_source(dx)
            arrived(piece(row, qs), px_s.at[dx, qs], px_r.at[dx, qs], {"row": row})
            for dy in range(1, B):
                send(piece(row, qs), fy_s.at[dy, dx, qs], fy_r.at[dy, dx, qs], {"row": y_peer(dy)})

    late = len(sends)
    for d in range(1, C):
        from_c = lax.rem(c - d + C, C)
        ref = grow.at[:, cols_of(from_c, l)]
        arrived(ref, gr_s.at[d], gr_r.at[d], {"col": from_c})
        send(ref, gs_s.at[d], gs_r.at[d], {"layer": sib})
    for d in range(C):
        from_c = lax.rem(c - d + C, C)
        arrived(grow.at[:, cols_of(from_c, sib)], gs_s.at[d], gs_r.at[d], {"layer": sib})

    for q in range(PIECES):
        acc[:, part(q)] -= 2.0 * by(grow, r, q)
    for dx in range(1, A):
        row = x_source(dx)
        for q in x_order:
            if q in first:
                arrived(piece(row, q), px_s.at[dx, q], px_r.at[dx, q], {"row": row})
            acc[:, part(q)] += term(row, q)
    for dy in range(1, B):
        row = y_source(dy)
        for q in y_order:
            if q in second:
                arrived(piece(row, q), py_s.at[dy, q], py_r.at[dy, q], {"row": row})
            acc[:, part(q)] += term(row, q)
    for copy in sends[:early] + sends[late:]:
        copy.wait_send()
    for qf, qs in zip(first, second):
        for q, s_sem, r_sem in ((qf, fx_s, fx_r), (qs, fy_s, fy_r)):
            for dy in range(1, B):
                for dx in range(1, A):
                    row = both_source(dy, dx)
                    arrived(piece(row, q), s_sem.at[dy, dx, q], r_sem.at[dy, dx, q], {"row": row})
            total = acc[:, part(q)]
            for dy in range(1, B):
                for dx in range(1, A):
                    row = both_source(dy, dx)
                    total = total + term(row, q)
            out_ref[:, part(q)] = total.astype(jnp.bfloat16)

    for copy in sends[early:late]:
        copy.wait_send()


def shards(R, C, L, density, panel, pattern):
    A = 1
    while A * A < R:
        A *= 2
    B = R // A
    tr, ti = density.shape
    half = ti // L
    W = panel.shape[1] // L
    K = tr * R
    dma = pltpu.SemaphoreType.DMA
    any_spec = pl.BlockSpec(memory_space=pl.ANY)
    bf16 = jnp.bfloat16
    return pl.pallas_call(
        functools.partial(kernel, (R, A, C)),
        out_shape=pltpu.VMEM((tr, W), bf16),
        in_specs=[any_spec] * 3,
        out_specs=pl.BlockSpec(memory_space=pltpu.VMEM),
        scratch_shapes=[
            pltpu.SMEM(pattern.shape, jnp.int32),
            pltpu.VMEM((tr, ti), bf16),
            pltpu.VMEM((K, half), bf16),
            pltpu.VMEM((tr, K), bf16),
            pltpu.VMEM((tr, K), bf16),
            pltpu.VMEM((R, tr, W), bf16),
            pltpu.VMEM((tr, W), jnp.float32),
            dma((3,)),
            dma((A,)), dma((A,)), dma((B,)), dma((B,)),
            dma((B, A)), dma((B, A)), dma((B, A)), dma((B, A)),
            dma((C,)), dma((C,)), dma((C,)), dma((C,)),
            dma((C,)), dma((C,)), dma((C,)), dma((C,)),
            dma((A, PIECES)), dma((A, PIECES)),
            dma((B, PIECES)), dma((B, PIECES)),
            dma((B, A, PIECES)), dma((B, A, PIECES)),
            dma((B, A, PIECES)), dma((B, A, PIECES)),
        ],
        compiler_params=pltpu.CompilerParams(
            collective_id=0, has_side_effects=True, vmem_limit_bytes=56 * 1024 * 1024
        ),
    )(density, panel, pattern)


def solution(mesh):
    R, C, L = mesh.shape["row"], mesh.shape["col"], mesh.shape["layer"]
    in_specs = (P("row", "col"), P("row", "col"), P("row", "col"))
    out_specs = P("row", ("col", "layer"))
    return jax.shard_map(
        functools.partial(shards, R, C, L),
        mesh=mesh, in_specs=in_specs, out_specs=out_specs, check_vma=False,
    )
```

```python
import functools

import jax
import jax.numpy as jnp
from jax import lax
from jax.experimental import pallas as pl
from jax.experimental.pallas import tpu as pltpu
from jax.sharding import PartitionSpec as P

BS = 128
PIECES = 4
MESH = pl.DeviceIdType.MESH


def kernel(
    sizes, density_ref, panel_ref, pattern_hbm, out_ref,
    pattern_ref, tile, fcol, frow, grow, p, acc,
    load_sem, cx_s, cx_r, cy_s, cy_r, ex_s, ex_r, ey_s, ey_r, fr_s, fr_r, fs_s, fs_r, gr_s, gr_r, gs_s, gs_r,
    px_s, px_r, py_s, py_r, fx_s, fx_r, fy_s, fy_r,
):
    R, A, C = sizes
    B = R // A
    tr, ti = density_ref.shape
    half = ti // 2
    W = p.shape[1]
    wq = W // PIECES
    r = lax.axis_index("row")
    c = lax.axis_index("col")
    l = lax.axis_index("layer")
    x = lax.rem(r, A)
    y = r // A
    sib = 1 - l

    def rem_copy(ref, ssem, rsem, dev):
        return pltpu.make_async_remote_copy(
            src_ref=ref, dst_ref=ref, send_sem=ssem, recv_sem=rsem,
            device_id=dev, device_id_type=MESH,
        )

    def x_peer(d):
        return y * A + lax.rem(x + d, A)

    def y_peer(d):
        return lax.rem(y + d, B) * A + x

    barrier = pltpu.get_barrier_semaphore()
    for d in range(1, A):
        pl.semaphore_signal(barrier, inc=1, device_id={"row": x_peer(d)}, device_id_type=MESH)
    for d in range(1, B):
        pl.semaphore_signal(barrier, inc=1, device_id={"row": y_peer(d)}, device_id_type=MESH)
    for d in range(1, C):
        pl.semaphore_signal(barrier, inc=1, device_id={"col": lax.rem(c + d, C)}, device_id_type=MESH)
    pl.semaphore_signal(barrier, inc=1, device_id={"layer": sib}, device_id_type=MESH)

    load_pattern = pltpu.make_async_copy(pattern_hbm, pattern_ref, load_sem.at[2])
    load_pattern.start()
    load_tile = pltpu.make_async_copy(density_ref, tile, load_sem.at[0])
    load_tile.start()
    own_cols = pl.ds(pl.multiple_of(l * W, W), W)
    load_panel = pltpu.make_async_copy(panel_ref.at[:, own_cols], p.at[0:tr, :], load_sem.at[1])
    load_panel.start()
    first, second = range(PIECES // 2), range(PIECES // 2, PIECES)

    def cols_of(col, layer, width=half, extra=0):
        at = col * ti + layer * half + extra
        row = at // tr
        dy, dx = lax.rem(y - row // A + B, B), lax.rem(x - lax.rem(row, A) + A, A)
        return pl.ds(pl.multiple_of((dy * A + dx) * tr + lax.rem(at, tr), width), width)

    def rows_of(slot):
        return slice(slot * tr, (slot + 1) * tr)

    def half_rows(slot, which):
        return fcol.at[slot * tr + which * (tr // 2):slot * tr + (which + 1) * (tr // 2), :]

    def piece(slot, q):
        return p.at[rows_of(slot), q * wq:(q + 1) * wq]

    def x_source(d):
        return y * A + lax.rem(x - d + A, A)

    def y_source(d):
        return lax.rem(y - d + B, B) * A + x

    sends = []

    def send(ref, ssem, rsem, dev, src=None):
        copy = pltpu.make_async_remote_copy(
            src_ref=ref if src is None else src, dst_ref=ref, send_sem=ssem, recv_sem=rsem,
            device_id=dev, device_id_type=MESH,
        )
        copy.start()
        sends.append(copy)

    def arrived(ref, ssem, rsem, dev):
        rem_copy(ref, ssem, rsem, dev).wait_recv()

    x_order = list(second) + list(first)
    y_order = list(first) + list(second)

    def send_own(n, from_hbm=False):
        def src(q):
            at = pl.ds(pl.multiple_of(l * W + q * wq, wq), wq)
            return panel_ref.at[:, at] if from_hbm else piece(0, q)
        qx, qy = x_order[n], y_order[n]
        for d in range(1, A):
            send(piece(d, qx), px_s.at[d, qx], px_r.at[d, qx], {"row": x_peer(d)}, src(qx))
        for d in range(1, B):
            send(piece(d * A, qy), py_s.at[d, qy], py_r.at[d, qy], {"row": y_peer(d)}, src(qy))

    pl.semaphore_wait(barrier, A - 1 + B - 1 + C - 1 + 1)
    send_own(0, from_hbm=True)

    load_pattern.wait()
    load_tile.wait()
    for a in range(tr // BS):
        for b in range(ti // BS):
            keep = pattern_ref[a, b].astype(jnp.float32)
            block = tile[a * BS:(a + 1) * BS, b * BS:(b + 1) * BS].astype(jnp.float32) * keep
            frow[a * BS:(a + 1) * BS, cols_of(c, 0, BS, b * BS)] = block.astype(jnp.bfloat16)
    for d in range(1, C):
        send(frow.at[:, cols_of(c, l)], fr_s.at[d], fr_r.at[d], {"col": lax.rem(c + d, C)})
    fcol[rows_of(0), :] = frow[:, cols_of(c, l)]
    own_rows = fcol.at[rows_of(0), :]
    for d in range(1, A):
        send(fcol.at[rows_of(d), :], cx_s.at[d], cx_r.at[d], {"row": x_peer(d)}, own_rows)
    for d in range(1, B):
        send(fcol.at[rows_of(d * A), :], cy_s.at[d], cy_r.at[d], {"row": y_peer(d)}, own_rows)
    load_panel.wait()
    send_own(1)

    for dy in range(1, B):
        arrived(fcol.at[rows_of(dy * A), :], cy_s.at[dy], cy_r.at[dy], {"row": y_source(dy)})
        for dx in range(1, A):
            send(half_rows(dy * A + dx, 0), ex_s.at[dy, dx], ex_r.at[dy, dx], {"row": x_peer(dx)},
                 half_rows(dy * A, 0))
    for dx in range(1, A):
        arrived(fcol.at[rows_of(dx), :], cx_s.at[dx], cx_r.at[dx], {"row": x_source(dx)})
        for dy in range(1, B):
            send(half_rows(dy * A + dx, 1), ey_s.at[dy, dx], ey_r.at[dy, dx], {"row": y_peer(dy)},
                 half_rows(dx, 1))
    for n in range(2, PIECES):
        send_own(n)

    for d in range(1, C):
        from_c = lax.rem(c - d + C, C)
        ref = frow.at[:, cols_of(from_c, l)]
        arrived(ref, fr_s.at[d], fr_r.at[d], {"col": from_c})
        send(ref, fs_s.at[d], fs_r.at[d], {"layer": sib})
    for d in range(1, C):
        from_c = lax.rem(c - d + C, C)
        arrived(frow.at[:, cols_of(from_c, sib)], fs_s.at[d], fs_r.at[d], {"layer": sib})
    for dy in range(1, B):
        for dx in range(1, A):
            slot = dy * A + dx
            arrived(half_rows(slot, 0), ex_s.at[dy, dx], ex_r.at[dy, dx], {"row": x_source(dx)})
            arrived(half_rows(slot, 1), ey_s.at[dy, dx], ey_r.at[dy, dx], {"row": y_source(dy)})

    grow[:, cols_of(c, l)] = jnp.dot(
        frow[...], fcol[...], preferred_element_type=jnp.float32
    ).astype(jnp.bfloat16)
    for d in range(1, C):
        send(grow.at[:, cols_of(c, l)], gr_s.at[d], gr_r.at[d], {"col": lax.rem(c + d, C)})
    send(grow.at[:, cols_of(c, l)], gs_s.at[0], gs_r.at[0], {"layer": sib})

    def part(q):
        return slice(q * wq, (q + 1) * wq)

    def by(left, group, q):
        at = slice(group[0] * tr, group[1] * tr)
        return jnp.dot(left[:, at], p[at, part(q)], preferred_element_type=jnp.float32)

    near = [(0, A)]
    for dy in range(1, B):
        if dy * A == near[-1][1]:
            near[-1] = (near[-1][0], dy * A + 1)
        else:
            near.append((dy * A, dy * A + 1))
    far = [(dy * A + 1, dy * A + A) for dy in range(1, B)]

    early = len(sends)
    for qf, qs in zip(first, second):
        for dy in range(1, B):
            arrived(piece(dy * A, qf), py_s.at[dy, qf], py_r.at[dy, qf], {"row": y_source(dy)})
            for dx in range(1, A):
                send(piece(dy * A + dx, qf), fx_s.at[dy, dx, qf], fx_r.at[dy, dx, qf],
                     {"row": x_peer(dx)}, piece(dy * A, qf))
        for dx in range(1, A):
            arrived(piece(dx, qs), px_s.at[dx, qs], px_r.at[dx, qs], {"row": x_source(dx)})
            for dy in range(1, B):
                send(piece(dy * A + dx, qs), fy_s.at[dy, dx, qs], fy_r.at[dy, dx, qs],
                     {"row": y_peer(dy)}, piece(dx, qs))
    late = len(sends)

    for d in range(1, C):
        from_c = lax.rem(c - d + C, C)
        ref = grow.at[:, cols_of(from_c, l)]
        arrived(ref, gr_s.at[d], gr_r.at[d], {"col": from_c})
        send(ref, gs_s.at[d], gs_r.at[d], {"layer": sib})
    for qf, qs in zip(first, second):
        for dy in range(1, B):
            arrived(piece(dy * A, qs), py_s.at[dy, qs], py_r.at[dy, qs], {"row": y_source(dy)})
        for dx in range(1, A):
            arrived(piece(dx, qf), px_s.at[dx, qf], px_r.at[dx, qf], {"row": x_source(dx)})
        for q in (qf, qs):
            acc[:, part(q)] = 3.0 * sum(by(frow, group, q) for group in near)
    for d in range(C):
        from_c = lax.rem(c - d + C, C)
        arrived(grow.at[:, cols_of(from_c, sib)], gs_s.at[d], gs_r.at[d], {"layer": sib})
    for q in range(PIECES):
        acc[:, part(q)] -= 2.0 * sum(by(grow, group, q) for group in near)

    for copy in sends[:early] + sends[late:]:
        copy.wait_send()
    for qf, qs in zip(first, second):
        for dy in range(1, B):
            for dx in range(1, A):
                slot = dy * A + dx
                arrived(piece(slot, qf), fx_s.at[dy, dx, qf], fx_r.at[dy, dx, qf], {"row": x_source(dx)})
                arrived(piece(slot, qs), fy_s.at[dy, dx, qs], fy_r.at[dy, dx, qs], {"row": y_source(dy)})
        for q in (qf, qs):
            total = acc[:, part(q)]
            for group in far:
                total = total + (3.0 * by(frow, group, q) - 2.0 * by(grow, group, q))
            out_ref[:, part(q)] = total.astype(jnp.bfloat16)

    for copy in sends[early:late]:
        copy.wait_send()


def shards(R, C, L, density, panel, pattern):
    A = 1
    while A * A < R:
        A *= 2
    B = R // A
    tr, ti = density.shape
    half = ti // L
    W = panel.shape[1] // L
    K = tr * R
    dma = pltpu.SemaphoreType.DMA
    any_spec = pl.BlockSpec(memory_space=pl.ANY)
    bf16 = jnp.bfloat16
    return pl.pallas_call(
        functools.partial(kernel, (R, A, C)),
        out_shape=pltpu.VMEM((tr, W), bf16),
        in_specs=[any_spec] * 3,
        out_specs=pl.BlockSpec(memory_space=pltpu.VMEM),
        scratch_shapes=[
            pltpu.SMEM(pattern.shape, jnp.int32),
            pltpu.VMEM((tr, ti), bf16),
            pltpu.VMEM((K, half), bf16),
            pltpu.VMEM((tr, K), bf16),
            pltpu.VMEM((tr, K), bf16),
            pltpu.VMEM((K, W), bf16),
            pltpu.VMEM((tr, W), jnp.float32),
            dma((3,)),
            dma((A,)), dma((A,)), dma((B,)), dma((B,)),
            dma((B, A)), dma((B, A)), dma((B, A)), dma((B, A)),
            dma((C,)), dma((C,)), dma((C,)), dma((C,)),
            dma((C,)), dma((C,)), dma((C,)), dma((C,)),
            dma((A, PIECES)), dma((A, PIECES)),
            dma((B, PIECES)), dma((B, PIECES)),
            dma((B, A, PIECES)), dma((B, A, PIECES)),
            dma((B, A, PIECES)), dma((B, A, PIECES)),
        ],
        compiler_params=pltpu.CompilerParams(
            collective_id=0, has_side_effects=True, vmem_limit_bytes=56 * 1024 * 1024
        ),
    )(density, panel, pattern)


def solution(mesh):
    R, C, L = mesh.shape["row"], mesh.shape["col"], mesh.shape["layer"]
    in_specs = (P("row", "col"), P("row", "col"), P("row", "col"))
    out_specs = P("row", ("col", "layer"))
    return jax.shard_map(
        functools.partial(shards, R, C, L),
        mesh=mesh, in_specs=in_specs, out_specs=out_specs, check_vma=False,
    )
```

```python
import functools

import jax
import jax.numpy as jnp
from jax import lax
from jax.experimental import pallas as pl
from jax.experimental.pallas import tpu as pltpu
from jax.sharding import PartitionSpec as P

BS = 128
PIECES = 4
MESH = pl.DeviceIdType.MESH


def kernel(
    sizes, density_ref, panel_ref, pattern_hbm, out_ref,
    pattern_ref, tile, fcol, frow, grow, p, acc,
    load_sem, cx_s, cx_r, cy_s, cy_r, ex_s, ex_r, ey_s, ey_r, fr_s, fr_r, fs_s, fs_r, gr_s, gr_r, gs_s, gs_r,
    px_s, px_r, py_s, py_r, fx_s, fx_r, fy_s, fy_r,
):
    R, A, C = sizes
    B = R // A
    tr, ti = density_ref.shape
    half = ti // 2
    W = p.shape[1]
    wq = W // PIECES
    r = lax.axis_index("row")
    c = lax.axis_index("col")
    l = lax.axis_index("layer")
    x = lax.rem(r, A)
    y = r // A
    sib = 1 - l

    def rem_copy(ref, ssem, rsem, dev):
        return pltpu.make_async_remote_copy(
            src_ref=ref, dst_ref=ref, send_sem=ssem, recv_sem=rsem,
            device_id=dev, device_id_type=MESH,
        )

    def x_peer(d):
        return y * A + lax.rem(x + d, A)

    def y_peer(d):
        return lax.rem(y + d, B) * A + x

    barrier = pltpu.get_barrier_semaphore()
    for d in range(1, A):
        pl.semaphore_signal(barrier, inc=1, device_id={"row": x_peer(d)}, device_id_type=MESH)
    for d in range(1, B):
        pl.semaphore_signal(barrier, inc=1, device_id={"row": y_peer(d)}, device_id_type=MESH)
    for d in range(1, C):
        pl.semaphore_signal(barrier, inc=1, device_id={"col": lax.rem(c + d, C)}, device_id_type=MESH)
    pl.semaphore_signal(barrier, inc=1, device_id={"layer": sib}, device_id_type=MESH)

    load_pattern = pltpu.make_async_copy(pattern_hbm, pattern_ref, load_sem.at[2])
    load_pattern.start()
    load_tile = pltpu.make_async_copy(density_ref, tile, load_sem.at[0])
    load_tile.start()
    own_cols = pl.ds(pl.multiple_of(l * W, W), W)
    load_panel = pltpu.make_async_copy(panel_ref.at[:, own_cols], p.at[0:tr, :], load_sem.at[1])
    load_panel.start()
    first, second = range(PIECES // 2), range(PIECES // 2, PIECES)

    def cols_of(col, layer, width=half, extra=0):
        at = col * ti + layer * half + extra
        row = at // tr
        dy, dx = lax.rem(y - row // A + B, B), lax.rem(x - lax.rem(row, A) + A, A)
        return pl.ds(pl.multiple_of((dy * A + dx) * tr + lax.rem(at, tr), width), width)

    def rows_of(slot):
        return slice(slot * tr, (slot + 1) * tr)

    def half_rows(slot, which):
        return fcol.at[slot * tr + which * (tr // 2):slot * tr + (which + 1) * (tr // 2), :]

    def piece(slot, q):
        return p.at[rows_of(slot), q * wq:(q + 1) * wq]

    def x_source(d):
        return y * A + lax.rem(x - d + A, A)

    def y_source(d):
        return lax.rem(y - d + B, B) * A + x

    sends = []

    def send(ref, ssem, rsem, dev, src=None):
        copy = pltpu.make_async_remote_copy(
            src_ref=ref if src is None else src, dst_ref=ref, send_sem=ssem, recv_sem=rsem,
            device_id=dev, device_id_type=MESH,
        )
        copy.start()
        sends.append(copy)

    def arrived(ref, ssem, rsem, dev):
        rem_copy(ref, ssem, rsem, dev).wait_recv()

    x_order = list(second) + list(first)
    y_order = list(first) + list(second)

    def send_own(n):
        qx, qy = x_order[n], y_order[n]
        for d in range(1, A):
            send(piece(d, qx), px_s.at[d, qx], px_r.at[d, qx], {"row": x_peer(d)}, piece(0, qx))
        for d in range(1, B):
            send(piece(d * A, qy), py_s.at[d, qy], py_r.at[d, qy], {"row": y_peer(d)}, piece(0, qy))

    load_pattern.wait()
    load_tile.wait()
    for a in range(tr // BS):
        for b in range(ti // BS):
            keep = pattern_ref[a, b].astype(jnp.float32)
            block = tile[a * BS:(a + 1) * BS, b * BS:(b + 1) * BS].astype(jnp.float32) * keep
            frow[a * BS:(a + 1) * BS, cols_of(c, 0, BS, b * BS)] = block.astype(jnp.bfloat16)
    fcol[rows_of(0), :] = frow[:, cols_of(c, l)]

    pl.semaphore_wait(barrier, A - 1 + B - 1 + C - 1 + 1)
    for d in range(1, C):
        send(frow.at[:, cols_of(c, l)], fr_s.at[d], fr_r.at[d], {"col": lax.rem(c + d, C)})
    own_rows = fcol.at[rows_of(0), :]
    for d in range(1, A):
        send(fcol.at[rows_of(d), :], cx_s.at[d], cx_r.at[d], {"row": x_peer(d)}, own_rows)
    for d in range(1, B):
        send(fcol.at[rows_of(d * A), :], cy_s.at[d], cy_r.at[d], {"row": y_peer(d)}, own_rows)
    load_panel.wait()
    send_own(0)
    send_own(1)

    for dy in range(1, B):
        arrived(fcol.at[rows_of(dy * A), :], cy_s.at[dy], cy_r.at[dy], {"row": y_source(dy)})
        for dx in range(1, A):
            send(half_rows(dy * A + dx, 0), ex_s.at[dy, dx], ex_r.at[dy, dx], {"row": x_peer(dx)},
                 half_rows(dy * A, 0))
    for dx in range(1, A):
        arrived(fcol.at[rows_of(dx), :], cx_s.at[dx], cx_r.at[dx], {"row": x_source(dx)})
        for dy in range(1, B):
            send(half_rows(dy * A + dx, 1), ey_s.at[dy, dx], ey_r.at[dy, dx], {"row": y_peer(dy)},
                 half_rows(dx, 1))
    for n in range(2, PIECES):
        send_own(n)

    for d in range(1, C):
        from_c = lax.rem(c - d + C, C)
        ref = frow.at[:, cols_of(from_c, l)]
        arrived(ref, fr_s.at[d], fr_r.at[d], {"col": from_c})
        send(ref, fs_s.at[d], fs_r.at[d], {"layer": sib})
    for d in range(1, C):
        from_c = lax.rem(c - d + C, C)
        arrived(frow.at[:, cols_of(from_c, sib)], fs_s.at[d], fs_r.at[d], {"layer": sib})
    for dy in range(1, B):
        for dx in range(1, A):
            slot = dy * A + dx
            arrived(half_rows(slot, 0), ex_s.at[dy, dx], ex_r.at[dy, dx], {"row": x_source(dx)})
            arrived(half_rows(slot, 1), ey_s.at[dy, dx], ey_r.at[dy, dx], {"row": y_source(dy)})

    grow[:, cols_of(c, l)] = jnp.dot(
        frow[...], fcol[...], preferred_element_type=jnp.float32
    ).astype(jnp.bfloat16)
    for d in range(1, C):
        send(grow.at[:, cols_of(c, l)], gr_s.at[d], gr_r.at[d], {"col": lax.rem(c + d, C)})
    send(grow.at[:, cols_of(c, l)], gs_s.at[0], gs_r.at[0], {"layer": sib})

    def part(q):
        return slice(q * wq, (q + 1) * wq)

    def by(left, group, q):
        at = slice(group[0] * tr, group[1] * tr)
        return jnp.dot(left[:, at], p[at, part(q)], preferred_element_type=jnp.float32)

    near = [(0, A)]
    for dy in range(1, B):
        if dy * A == near[-1][1]:
            near[-1] = (near[-1][0], dy * A + 1)
        else:
            near.append((dy * A, dy * A + 1))
    far = [(dy * A + 1, dy * A + A) for dy in range(1, B)]

    early = len(sends)
    for qf, qs in zip(first, second):
        for dy in range(1, B):
            arrived(piece(dy * A, qf), py_s.at[dy, qf], py_r.at[dy, qf], {"row": y_source(dy)})
            for dx in range(1, A):
                send(piece(dy * A + dx, qf), fx_s.at[dy, dx, qf], fx_r.at[dy, dx, qf],
                     {"row": x_peer(dx)}, piece(dy * A, qf))
        for dx in range(1, A):
            arrived(piece(dx, qs), px_s.at[dx, qs], px_r.at[dx, qs], {"row": x_source(dx)})
            for dy in range(1, B):
                send(piece(dy * A + dx, qs), fy_s.at[dy, dx, qs], fy_r.at[dy, dx, qs],
                     {"row": y_peer(dy)}, piece(dx, qs))
    late = len(sends)

    for d in range(1, C):
        from_c = lax.rem(c - d + C, C)
        ref = grow.at[:, cols_of(from_c, l)]
        arrived(ref, gr_s.at[d], gr_r.at[d], {"col": from_c})
        send(ref, gs_s.at[d], gs_r.at[d], {"layer": sib})
    for qf, qs in zip(first, second):
        for dy in range(1, B):
            arrived(piece(dy * A, qs), py_s.at[dy, qs], py_r.at[dy, qs], {"row": y_source(dy)})
        for dx in range(1, A):
            arrived(piece(dx, qf), px_s.at[dx, qf], px_r.at[dx, qf], {"row": x_source(dx)})
        for q in (qf, qs):
            acc[:, part(q)] = 3.0 * sum(by(frow, group, q) for group in near)
    for d in range(C):
        from_c = lax.rem(c - d + C, C)
        arrived(grow.at[:, cols_of(from_c, sib)], gs_s.at[d], gs_r.at[d], {"layer": sib})
    for q in range(PIECES):
        acc[:, part(q)] -= 2.0 * sum(by(grow, group, q) for group in near)

    for copy in sends[:early] + sends[late:]:
        copy.wait_send()
    for qf, qs in zip(first, second):
        for dy in range(1, B):
            for dx in range(1, A):
                slot = dy * A + dx
                arrived(piece(slot, qf), fx_s.at[dy, dx, qf], fx_r.at[dy, dx, qf], {"row": x_source(dx)})
                arrived(piece(slot, qs), fy_s.at[dy, dx, qs], fy_r.at[dy, dx, qs], {"row": y_source(dy)})
        for q in (qf, qs):
            total = acc[:, part(q)]
            for group in far:
                total = total + (3.0 * by(frow, group, q) - 2.0 * by(grow, group, q))
            out_ref[:, part(q)] = total.astype(jnp.bfloat16)

    for copy in sends[early:late]:
        copy.wait_send()


def shards(R, C, L, density, panel, pattern):
    A = 1
    while A * A < R:
        A *= 2
    B = R // A
    tr, ti = density.shape
    half = ti // L
    W = panel.shape[1] // L
    K = tr * R
    dma = pltpu.SemaphoreType.DMA
    any_spec = pl.BlockSpec(memory_space=pl.ANY)
    bf16 = jnp.bfloat16
    return pl.pallas_call(
        functools.partial(kernel, (R, A, C)),
        out_shape=pltpu.VMEM((tr, W), bf16),
        in_specs=[any_spec] * 3,
        out_specs=pl.BlockSpec(memory_space=pltpu.VMEM),
        scratch_shapes=[
            pltpu.SMEM(pattern.shape, jnp.int32),
            pltpu.VMEM((tr, ti), bf16),
            pltpu.VMEM((K, half), bf16),
            pltpu.VMEM((tr, K), bf16),
            pltpu.VMEM((tr, K), bf16),
            pltpu.VMEM((K, W), bf16),
            pltpu.VMEM((tr, W), jnp.float32),
            dma((3,)),
            dma((A,)), dma((A,)), dma((B,)), dma((B,)),
            dma((B, A)), dma((B, A)), dma((B, A)), dma((B, A)),
            dma((C,)), dma((C,)), dma((C,)), dma((C,)),
            dma((C,)), dma((C,)), dma((C,)), dma((C,)),
            dma((A, PIECES)), dma((A, PIECES)),
            dma((B, PIECES)), dma((B, PIECES)),
            dma((B, A, PIECES)), dma((B, A, PIECES)),
            dma((B, A, PIECES)), dma((B, A, PIECES)),
        ],
        compiler_params=pltpu.CompilerParams(
            collective_id=0, has_side_effects=True, vmem_limit_bytes=56 * 1024 * 1024
        ),
    )(density, panel, pattern)


def solution(mesh):
    R, C, L = mesh.shape["row"], mesh.shape["col"], mesh.shape["layer"]
    in_specs = (P("row", "col"), P("row", "col"), P("row", "col"))
    out_specs = P("row", ("col", "layer"))
    return jax.shard_map(
        functools.partial(shards, R, C, L),
        mesh=mesh, in_specs=in_specs, out_specs=out_specs, check_vma=False,
    )
```

```python
import functools

import jax
import jax.numpy as jnp
from jax import lax
from jax.experimental import pallas as pl
from jax.experimental.pallas import tpu as pltpu
from jax.sharding import PartitionSpec as P

BS = 128
PIECES = 4
MESH = pl.DeviceIdType.MESH


def kernel(
    sizes, density_ref, panel_ref, pattern_hbm, out_ref,
    pattern_ref, tile, fcol, frow, grow, p, acc,
    load_sem, cx_s, cx_r, cy_s, cy_r, ex_s, ex_r, ey_s, ey_r, fr_s, fr_r, fs_s, fs_r, gr_s, gr_r, gs_s, gs_r,
    px_s, px_r, py_s, py_r, fx_s, fx_r, fy_s, fy_r,
):
    R, A, C = sizes
    B = R // A
    tr, ti = density_ref.shape
    half = ti // 2
    wq = p.shape[2]
    W = wq * PIECES
    r = lax.axis_index("row")
    c = lax.axis_index("col")
    l = lax.axis_index("layer")
    x = lax.rem(r, A)
    y = r // A
    sib = 1 - l

    def rem_copy(ref, ssem, rsem, dev):
        return pltpu.make_async_remote_copy(
            src_ref=ref, dst_ref=ref, send_sem=ssem, recv_sem=rsem,
            device_id=dev, device_id_type=MESH,
        )

    def x_peer(d):
        return y * A + lax.rem(x + d, A)

    def y_peer(d):
        return lax.rem(y + d, B) * A + x

    barrier = pltpu.get_barrier_semaphore()
    for d in range(1, A):
        pl.semaphore_signal(barrier, inc=1, device_id={"row": x_peer(d)}, device_id_type=MESH)
    for d in range(1, B):
        pl.semaphore_signal(barrier, inc=1, device_id={"row": y_peer(d)}, device_id_type=MESH)
    for d in range(1, C):
        pl.semaphore_signal(barrier, inc=1, device_id={"col": lax.rem(c + d, C)}, device_id_type=MESH)
    pl.semaphore_signal(barrier, inc=1, device_id={"layer": sib}, device_id_type=MESH)

    load_pattern = pltpu.make_async_copy(pattern_hbm, pattern_ref, load_sem.at[1])
    load_pattern.start()
    load_tile = pltpu.make_async_copy(density_ref, tile, load_sem.at[0])
    load_tile.start()
    load_panel = []
    for q in range(PIECES):
        at = pl.ds(pl.multiple_of(l * W + q * wq, wq), wq)
        load_panel.append(pltpu.make_async_copy(panel_ref.at[:, at], p.at[q, 0:tr, :], load_sem.at[2 + q]))
        load_panel[q].start()
    first, second = range(PIECES // 2), range(PIECES // 2, PIECES)

    def cols_of(col, layer, width=half, extra=0):
        at = col * ti + layer * half + extra
        row = at // tr
        dy, dx = lax.rem(y - row // A + B, B), lax.rem(x - lax.rem(row, A) + A, A)
        return pl.ds(pl.multiple_of((dy * A + dx) * tr + lax.rem(at, tr), width), width)

    def rows_of(slot):
        return slice(slot * tr, (slot + 1) * tr)

    def half_rows(slot, which):
        return fcol.at[slot * tr + which * (tr // 2):slot * tr + (which + 1) * (tr // 2), :]

    def piece(slot, q):
        return p.at[q, rows_of(slot), :]

    def x_source(d):
        return y * A + lax.rem(x - d + A, A)

    def y_source(d):
        return lax.rem(y - d + B, B) * A + x

    sends = []

    def send(ref, ssem, rsem, dev, src=None):
        copy = pltpu.make_async_remote_copy(
            src_ref=ref if src is None else src, dst_ref=ref, send_sem=ssem, recv_sem=rsem,
            device_id=dev, device_id_type=MESH,
        )
        copy.start()
        sends.append(copy)

    def arrived(ref, ssem, rsem, dev):
        rem_copy(ref, ssem, rsem, dev).wait_recv()

    x_order = list(second) + list(first)
    y_order = list(first) + list(second)

    def send_own(n):
        qx, qy = x_order[n], y_order[n]
        for d in range(1, A):
            send(piece(d, qx), px_s.at[d, qx], px_r.at[d, qx], {"row": x_peer(d)}, piece(0, qx))
        for d in range(1, B):
            send(piece(d * A, qy), py_s.at[d, qy], py_r.at[d, qy], {"row": y_peer(d)}, piece(0, qy))

    load_pattern.wait()
    load_tile.wait()
    for a in range(tr // BS):
        for b in range(ti // BS):
            keep = pattern_ref[a, b].astype(jnp.float32)
            block = tile[a * BS:(a + 1) * BS, b * BS:(b + 1) * BS].astype(jnp.float32) * keep
            frow[a * BS:(a + 1) * BS, cols_of(c, 0, BS, b * BS)] = block.astype(jnp.bfloat16)
    fcol[rows_of(0), :] = frow[:, cols_of(c, l)]

    pl.semaphore_wait(barrier, A - 1 + B - 1 + C - 1 + 1)
    for d in range(1, C):
        send(frow.at[:, cols_of(c, l)], fr_s.at[d], fr_r.at[d], {"col": lax.rem(c + d, C)})
    own_rows = fcol.at[rows_of(0), :]
    for d in range(1, A):
        send(fcol.at[rows_of(d), :], cx_s.at[d], cx_r.at[d], {"row": x_peer(d)}, own_rows)
    for d in range(1, B):
        send(fcol.at[rows_of(d * A), :], cy_s.at[d], cy_r.at[d], {"row": y_peer(d)}, own_rows)
    for copy in load_panel:
        copy.wait()
    send_own(0)
    send_own(1)

    for dy in range(1, B):
        arrived(fcol.at[rows_of(dy * A), :], cy_s.at[dy], cy_r.at[dy], {"row": y_source(dy)})
        for dx in range(1, A):
            send(half_rows(dy * A + dx, 0), ex_s.at[dy, dx], ex_r.at[dy, dx], {"row": x_peer(dx)},
                 half_rows(dy * A, 0))
    for dx in range(1, A):
        arrived(fcol.at[rows_of(dx), :], cx_s.at[dx], cx_r.at[dx], {"row": x_source(dx)})
        for dy in range(1, B):
            send(half_rows(dy * A + dx, 1), ey_s.at[dy, dx], ey_r.at[dy, dx], {"row": y_peer(dy)},
                 half_rows(dx, 1))
    for n in range(2, PIECES):
        send_own(n)

    for d in range(1, C):
        from_c = lax.rem(c - d + C, C)
        ref = frow.at[:, cols_of(from_c, l)]
        arrived(ref, fr_s.at[d], fr_r.at[d], {"col": from_c})
        send(ref, fs_s.at[d], fs_r.at[d], {"layer": sib})
    for d in range(1, C):
        from_c = lax.rem(c - d + C, C)
        arrived(frow.at[:, cols_of(from_c, sib)], fs_s.at[d], fs_r.at[d], {"layer": sib})
    for dy in range(1, B):
        for dx in range(1, A):
            slot = dy * A + dx
            arrived(half_rows(slot, 0), ex_s.at[dy, dx], ex_r.at[dy, dx], {"row": x_source(dx)})
            arrived(half_rows(slot, 1), ey_s.at[dy, dx], ey_r.at[dy, dx], {"row": y_source(dy)})

    grow[:, cols_of(c, l)] = jnp.dot(
        frow[...], fcol[...], preferred_element_type=jnp.float32
    ).astype(jnp.bfloat16)
    for d in range(1, C):
        send(grow.at[:, cols_of(c, l)], gr_s.at[d], gr_r.at[d], {"col": lax.rem(c + d, C)})
    send(grow.at[:, cols_of(c, l)], gs_s.at[0], gs_r.at[0], {"layer": sib})

    def part(q):
        return slice(q * wq, (q + 1) * wq)

    def by(left, group, q):
        at = slice(group[0] * tr, group[1] * tr)
        return jnp.dot(left[:, at], p[q, at, :], preferred_element_type=jnp.float32)

    near = [(0, A)]
    for dy in range(1, B):
        if dy * A == near[-1][1]:
            near[-1] = (near[-1][0], dy * A + 1)
        else:
            near.append((dy * A, dy * A + 1))
    far = [(dy * A + 1, dy * A + A) for dy in range(1, B)]

    early = len(sends)
    for qf, qs in zip(first, second):
        for dy in range(1, B):
            arrived(piece(dy * A, qf), py_s.at[dy, qf], py_r.at[dy, qf], {"row": y_source(dy)})
            for dx in range(1, A):
                send(piece(dy * A + dx, qf), fx_s.at[dy, dx, qf], fx_r.at[dy, dx, qf],
                     {"row": x_peer(dx)}, piece(dy * A, qf))
        for dx in range(1, A):
            arrived(piece(dx, qs), px_s.at[dx, qs], px_r.at[dx, qs], {"row": x_source(dx)})
            for dy in range(1, B):
                send(piece(dy * A + dx, qs), fy_s.at[dy, dx, qs], fy_r.at[dy, dx, qs],
                     {"row": y_peer(dy)}, piece(dx, qs))
    late = len(sends)

    for d in range(1, C):
        from_c = lax.rem(c - d + C, C)
        ref = grow.at[:, cols_of(from_c, l)]
        arrived(ref, gr_s.at[d], gr_r.at[d], {"col": from_c})
        send(ref, gs_s.at[d], gs_r.at[d], {"layer": sib})
    for qf, qs in zip(first, second):
        for dy in range(1, B):
            arrived(piece(dy * A, qs), py_s.at[dy, qs], py_r.at[dy, qs], {"row": y_source(dy)})
        for dx in range(1, A):
            arrived(piece(dx, qf), px_s.at[dx, qf], px_r.at[dx, qf], {"row": x_source(dx)})
        for q in (qf, qs):
            acc[:, part(q)] = 3.0 * sum(by(frow, group, q) for group in near)
    for d in range(C):
        from_c = lax.rem(c - d + C, C)
        arrived(grow.at[:, cols_of(from_c, sib)], gs_s.at[d], gs_r.at[d], {"layer": sib})
    for q in range(PIECES):
        acc[:, part(q)] -= 2.0 * sum(by(grow, group, q) for group in near)

    for copy in sends[:early] + sends[late:]:
        copy.wait_send()
    for qf, qs in zip(first, second):
        for dy in range(1, B):
            for dx in range(1, A):
                slot = dy * A + dx
                arrived(piece(slot, qf), fx_s.at[dy, dx, qf], fx_r.at[dy, dx, qf], {"row": x_source(dx)})
                arrived(piece(slot, qs), fy_s.at[dy, dx, qs], fy_r.at[dy, dx, qs], {"row": y_source(dy)})
        for q in (qf, qs):
            total = acc[:, part(q)]
            for group in far:
                total = total + (3.0 * by(frow, group, q) - 2.0 * by(grow, group, q))
            out_ref[:, part(q)] = total.astype(jnp.bfloat16)

    for copy in sends[early:late]:
        copy.wait_send()


def shards(R, C, L, density, panel, pattern):
    A = 1
    while A * A < R:
        A *= 2
    B = R // A
    tr, ti = density.shape
    half = ti // L
    W = panel.shape[1] // L
    K = tr * R
    dma = pltpu.SemaphoreType.DMA
    any_spec = pl.BlockSpec(memory_space=pl.ANY)
    bf16 = jnp.bfloat16
    return pl.pallas_call(
        functools.partial(kernel, (R, A, C)),
        out_shape=pltpu.VMEM((tr, W), bf16),
        in_specs=[any_spec] * 3,
        out_specs=pl.BlockSpec(memory_space=pltpu.VMEM),
        scratch_shapes=[
            pltpu.SMEM(pattern.shape, jnp.int32),
            pltpu.VMEM((tr, ti), bf16),
            pltpu.VMEM((K, half), bf16),
            pltpu.VMEM((tr, K), bf16),
            pltpu.VMEM((tr, K), bf16),
            pltpu.VMEM((PIECES, K, W // PIECES), bf16),
            pltpu.VMEM((tr, W), jnp.float32),
            dma((2 + PIECES,)),
            dma((A,)), dma((A,)), dma((B,)), dma((B,)),
            dma((B, A)), dma((B, A)), dma((B, A)), dma((B, A)),
            dma((C,)), dma((C,)), dma((C,)), dma((C,)),
            dma((C,)), dma((C,)), dma((C,)), dma((C,)),
            dma((A, PIECES)), dma((A, PIECES)),
            dma((B, PIECES)), dma((B, PIECES)),
            dma((B, A, PIECES)), dma((B, A, PIECES)),
            dma((B, A, PIECES)), dma((B, A, PIECES)),
        ],
        compiler_params=pltpu.CompilerParams(
            collective_id=0, has_side_effects=True, vmem_limit_bytes=56 * 1024 * 1024
        ),
    )(density, panel, pattern)


def solution(mesh):
    R, C, L = mesh.shape["row"], mesh.shape["col"], mesh.shape["layer"]
    in_specs = (P("row", "col"), P("row", "col"), P("row", "col"))
    out_specs = P("row", ("col", "layer"))
    return jax.shard_map(
        functools.partial(shards, R, C, L),
        mesh=mesh, in_specs=in_specs, out_specs=out_specs, check_vma=False,
    )
```

```python
import functools

import jax
import jax.numpy as jnp
from jax import lax
from jax.experimental import pallas as pl
from jax.experimental.pallas import tpu as pltpu
from jax.sharding import PartitionSpec as P

BS = 128
PIECES = 4
MESH = pl.DeviceIdType.MESH


def kernel(
    sizes, density_ref, panel_ref, pattern_hbm, out_ref,
    pattern_ref, tile, fcol, frow, grow, p, acc,
    load_sem, cx_s, cx_r, cy_s, cy_r, ex_s, ex_r, ey_s, ey_r, fr_s, fr_r, fs_s, fs_r, gr_s, gr_r, gs_s, gs_r,
    px_s, px_r, py_s, py_r, fx_s, fx_r, fy_s, fy_r,
):
    R, A, C = sizes
    B = R // A
    tr, ti = density_ref.shape
    half = ti // 2
    wq = p.shape[2]
    W = wq * PIECES
    r = lax.axis_index("row")
    c = lax.axis_index("col")
    l = lax.axis_index("layer")
    x = lax.rem(r, A)
    y = r // A
    sib = 1 - l

    def rem_copy(ref, ssem, rsem, dev):
        return pltpu.make_async_remote_copy(
            src_ref=ref, dst_ref=ref, send_sem=ssem, recv_sem=rsem,
            device_id=dev, device_id_type=MESH,
        )

    def x_peer(d):
        return y * A + lax.rem(x + d, A)

    def y_peer(d):
        return lax.rem(y + d, B) * A + x

    barrier = pltpu.get_barrier_semaphore()
    for d in range(1, A):
        pl.semaphore_signal(barrier, inc=1, device_id={"row": x_peer(d)}, device_id_type=MESH)
    for d in range(1, B):
        pl.semaphore_signal(barrier, inc=1, device_id={"row": y_peer(d)}, device_id_type=MESH)
    for d in range(1, C):
        pl.semaphore_signal(barrier, inc=1, device_id={"col": lax.rem(c + d, C)}, device_id_type=MESH)
    pl.semaphore_signal(barrier, inc=1, device_id={"layer": sib}, device_id_type=MESH)

    load_pattern = pltpu.make_async_copy(pattern_hbm, pattern_ref, load_sem.at[1])
    load_pattern.start()
    load_tile = pltpu.make_async_copy(density_ref, tile, load_sem.at[0])
    load_tile.start()
    load_panel = []
    for q in range(PIECES):
        at = pl.ds(pl.multiple_of(l * W + q * wq, wq), wq)
        load_panel.append(pltpu.make_async_copy(panel_ref.at[:, at], p.at[q, 0:tr, :], load_sem.at[2 + q]))
        load_panel[q].start()
    first, second = range(PIECES // 2), range(PIECES // 2, PIECES)

    def cols_of(col, layer, width=half, extra=0):
        at = col * ti + layer * half + extra
        row = at // tr
        dy, dx = lax.rem(y - row // A + B, B), lax.rem(x - lax.rem(row, A) + A, A)
        return pl.ds(pl.multiple_of((dy * A + dx) * tr + lax.rem(at, tr), width), width)

    def rows_of(slot):
        return slice(slot * tr, (slot + 1) * tr)

    def half_rows(slot, which):
        return fcol.at[slot * tr + which * (tr // 2):slot * tr + (which + 1) * (tr // 2), :]

    def piece(slot, q):
        return p.at[q, rows_of(slot), :]

    def x_source(d):
        return y * A + lax.rem(x - d + A, A)

    def y_source(d):
        return lax.rem(y - d + B, B) * A + x

    sends = []

    def send(ref, ssem, rsem, dev, src=None):
        copy = pltpu.make_async_remote_copy(
            src_ref=ref if src is None else src, dst_ref=ref, send_sem=ssem, recv_sem=rsem,
            device_id=dev, device_id_type=MESH,
        )
        copy.start()
        sends.append(copy)

    def arrived(ref, ssem, rsem, dev):
        rem_copy(ref, ssem, rsem, dev).wait_recv()

    x_order = list(second) + list(first)
    y_order = list(first) + list(second)

    def send_own(n):
        qx, qy = x_order[n], y_order[n]
        for d in range(1, A):
            send(piece(d, qx), px_s.at[d, qx], px_r.at[d, qx], {"row": x_peer(d)}, piece(0, qx))
        for d in range(1, B):
            send(piece(d * A, qy), py_s.at[d, qy], py_r.at[d, qy], {"row": y_peer(d)}, piece(0, qy))

    load_pattern.wait()
    load_tile.wait()
    for a in range(tr // BS):
        for b in range(ti // BS):
            keep = pattern_ref[a, b].astype(jnp.float32)
            block = tile[a * BS:(a + 1) * BS, b * BS:(b + 1) * BS].astype(jnp.float32) * keep
            frow[a * BS:(a + 1) * BS, cols_of(c, 0, BS, b * BS)] = block.astype(jnp.bfloat16)
    fcol[rows_of(0), :] = frow[:, cols_of(c, l)]

    pl.semaphore_wait(barrier, A - 1 + B - 1 + C - 1 + 1)
    for d in range(1, C):
        send(frow.at[:, cols_of(c, l)], fr_s.at[d], fr_r.at[d], {"col": lax.rem(c + d, C)})
    own_rows = fcol.at[rows_of(0), :]
    for d in range(1, A):
        send(fcol.at[rows_of(d), :], cx_s.at[d], cx_r.at[d], {"row": x_peer(d)}, own_rows)
    for d in range(1, B):
        send(fcol.at[rows_of(d * A), :], cy_s.at[d], cy_r.at[d], {"row": y_peer(d)}, own_rows)
    for copy in load_panel:
        copy.wait()
    send_own(0)
    send_own(1)

    for dy in range(1, B):
        arrived(fcol.at[rows_of(dy * A), :], cy_s.at[dy], cy_r.at[dy], {"row": y_source(dy)})
        for dx in range(1, A):
            send(half_rows(dy * A + dx, 0), ex_s.at[dy, dx], ex_r.at[dy, dx], {"row": x_peer(dx)},
                 half_rows(dy * A, 0))
    for dx in range(1, A):
        arrived(fcol.at[rows_of(dx), :], cx_s.at[dx], cx_r.at[dx], {"row": x_source(dx)})
        for dy in range(1, B):
            send(half_rows(dy * A + dx, 1), ey_s.at[dy, dx], ey_r.at[dy, dx], {"row": y_peer(dy)},
                 half_rows(dx, 1))
    for n in range(2, PIECES - 1):
        send_own(n)

    for d in range(1, C):
        from_c = lax.rem(c - d + C, C)
        ref = frow.at[:, cols_of(from_c, l)]
        arrived(ref, fr_s.at[d], fr_r.at[d], {"col": from_c})
        send(ref, fs_s.at[d], fs_r.at[d], {"layer": sib})
    send_own(PIECES - 1)
    for d in range(1, C):
        from_c = lax.rem(c - d + C, C)
        arrived(frow.at[:, cols_of(from_c, sib)], fs_s.at[d], fs_r.at[d], {"layer": sib})
    for dy in range(1, B):
        for dx in range(1, A):
            slot = dy * A + dx
            arrived(half_rows(slot, 0), ex_s.at[dy, dx], ex_r.at[dy, dx], {"row": x_source(dx)})
            arrived(half_rows(slot, 1), ey_s.at[dy, dx], ey_r.at[dy, dx], {"row": y_source(dy)})

    grow[:, cols_of(c, l)] = jnp.dot(
        frow[...], fcol[...], preferred_element_type=jnp.float32
    ).astype(jnp.bfloat16)
    for d in range(1, C):
        send(grow.at[:, cols_of(c, l)], gr_s.at[d], gr_r.at[d], {"col": lax.rem(c + d, C)})
    send(grow.at[:, cols_of(c, l)], gs_s.at[0], gs_r.at[0], {"layer": sib})

    def part(q):
        return slice(q * wq, (q + 1) * wq)

    def by(left, group, q):
        at = slice(group[0] * tr, group[1] * tr)
        return jnp.dot(left[:, at], p[q, at, :], preferred_element_type=jnp.float32)

    near = [(0, A)]
    for dy in range(1, B):
        if dy * A == near[-1][1]:
            near[-1] = (near[-1][0], dy * A + 1)
        else:
            near.append((dy * A, dy * A + 1))
    far = [(dy * A + 1, dy * A + A) for dy in range(1, B)]

    early = len(sends)
    for qf, qs in zip(first, second):
        for dy in range(1, B):
            arrived(piece(dy * A, qf), py_s.at[dy, qf], py_r.at[dy, qf], {"row": y_source(dy)})
            for dx in range(1, A):
                send(piece(dy * A + dx, qf), fx_s.at[dy, dx, qf], fx_r.at[dy, dx, qf],
                     {"row": x_peer(dx)}, piece(dy * A, qf))
        for dx in range(1, A):
            arrived(piece(dx, qs), px_s.at[dx, qs], px_r.at[dx, qs], {"row": x_source(dx)})
            for dy in range(1, B):
                send(piece(dy * A + dx, qs), fy_s.at[dy, dx, qs], fy_r.at[dy, dx, qs],
                     {"row": y_peer(dy)}, piece(dx, qs))
    late = len(sends)

    for d in range(1, C):
        from_c = lax.rem(c - d + C, C)
        ref = grow.at[:, cols_of(from_c, l)]
        arrived(ref, gr_s.at[d], gr_r.at[d], {"col": from_c})
        send(ref, gs_s.at[d], gs_r.at[d], {"layer": sib})
    for qf, qs in zip(first, second):
        for dy in range(1, B):
            arrived(piece(dy * A, qs), py_s.at[dy, qs], py_r.at[dy, qs], {"row": y_source(dy)})
        for dx in range(1, A):
            arrived(piece(dx, qf), px_s.at[dx, qf], px_r.at[dx, qf], {"row": x_source(dx)})
        for q in (qf, qs):
            acc[:, part(q)] = 3.0 * sum(by(frow, group, q) for group in near)
    for d in range(C):
        from_c = lax.rem(c - d + C, C)
        arrived(grow.at[:, cols_of(from_c, sib)], gs_s.at[d], gs_r.at[d], {"layer": sib})
    for q in range(PIECES):
        acc[:, part(q)] -= 2.0 * sum(by(grow, group, q) for group in near)

    for copy in sends[:early] + sends[late:]:
        copy.wait_send()
    for qf, qs in zip(first, second):
        for dy in range(1, B):
            for dx in range(1, A):
                slot = dy * A + dx
                arrived(piece(slot, qf), fx_s.at[dy, dx, qf], fx_r.at[dy, dx, qf], {"row": x_source(dx)})
                arrived(piece(slot, qs), fy_s.at[dy, dx, qs], fy_r.at[dy, dx, qs], {"row": y_source(dy)})
        for q in (qf, qs):
            total = acc[:, part(q)]
            for group in far:
                total = total + (3.0 * by(frow, group, q) - 2.0 * by(grow, group, q))
            out_ref[:, part(q)] = total.astype(jnp.bfloat16)

    for copy in sends[early:late]:
        copy.wait_send()


def shards(R, C, L, density, panel, pattern):
    A = 1
    while A * A < R:
        A *= 2
    B = R // A
    tr, ti = density.shape
    half = ti // L
    W = panel.shape[1] // L
    K = tr * R
    dma = pltpu.SemaphoreType.DMA
    any_spec = pl.BlockSpec(memory_space=pl.ANY)
    bf16 = jnp.bfloat16
    return pl.pallas_call(
        functools.partial(kernel, (R, A, C)),
        out_shape=pltpu.VMEM((tr, W), bf16),
        in_specs=[any_spec] * 3,
        out_specs=pl.BlockSpec(memory_space=pltpu.VMEM),
        scratch_shapes=[
            pltpu.SMEM(pattern.shape, jnp.int32),
            pltpu.VMEM((tr, ti), bf16),
            pltpu.VMEM((K, half), bf16),
            pltpu.VMEM((tr, K), bf16),
            pltpu.VMEM((tr, K), bf16),
            pltpu.VMEM((PIECES, K, W // PIECES), bf16),
            pltpu.VMEM((tr, W), jnp.float32),
            dma((2 + PIECES,)),
            dma((A,)), dma((A,)), dma((B,)), dma((B,)),
            dma((B, A)), dma((B, A)), dma((B, A)), dma((B, A)),
            dma((C,)), dma((C,)), dma((C,)), dma((C,)),
            dma((C,)), dma((C,)), dma((C,)), dma((C,)),
            dma((A, PIECES)), dma((A, PIECES)),
            dma((B, PIECES)), dma((B, PIECES)),
            dma((B, A, PIECES)), dma((B, A, PIECES)),
            dma((B, A, PIECES)), dma((B, A, PIECES)),
        ],
        compiler_params=pltpu.CompilerParams(
            collective_id=0, has_side_effects=True, vmem_limit_bytes=56 * 1024 * 1024
        ),
    )(density, panel, pattern)


def solution(mesh):
    R, C, L = mesh.shape["row"], mesh.shape["col"], mesh.shape["layer"]
    in_specs = (P("row", "col"), P("row", "col"), P("row", "col"))
    out_specs = P("row", ("col", "layer"))
    return jax.shard_map(
        functools.partial(shards, R, C, L),
        mesh=mesh, in_specs=in_specs, out_specs=out_specs, check_vma=False,
    )
```

```python
import functools

import jax
import jax.numpy as jnp
from jax import lax
from jax.experimental import pallas as pl
from jax.experimental.pallas import tpu as pltpu
from jax.sharding import PartitionSpec as P

BS = 128
PIECES = 4
MESH = pl.DeviceIdType.MESH


def kernel(
    sizes, density_ref, panel_ref, pattern_hbm, out_ref,
    pattern_ref, tile, fcol, frow, grow, p, acc,
    load_sem, cx_s, cx_r, cy_s, cy_r, ex_s, ex_r, ey_s, ey_r, cs_s, cs_r, fr_s, fr_r, fs_s, fs_r, gr_s, gr_r, gs_s, gs_r,
    px_s, px_r, py_s, py_r, fx_s, fx_r, fy_s, fy_r,
):
    R, A, C = sizes
    B = R // A
    tr, ti = density_ref.shape
    half = ti // 2
    hr = tr // 2
    block = min(ti, tr)
    blocks = range(ti // block)
    wq = p.shape[2]
    W = wq * PIECES
    r = lax.axis_index("row")
    c = lax.axis_index("col")
    l = lax.axis_index("layer")
    x = lax.rem(r, A)
    y = r // A
    sib = 1 - l

    def rem_copy(ref, ssem, rsem, dev):
        return pltpu.make_async_remote_copy(
            src_ref=ref, dst_ref=ref, send_sem=ssem, recv_sem=rsem,
            device_id=dev, device_id_type=MESH,
        )

    def x_peer(d):
        return y * A + lax.rem(x + d, A)

    def y_peer(d):
        return lax.rem(y + d, B) * A + x

    barrier = pltpu.get_barrier_semaphore()
    for d in range(1, A):
        pl.semaphore_signal(barrier, inc=1, device_id={"row": x_peer(d)}, device_id_type=MESH)
    for d in range(1, B):
        pl.semaphore_signal(barrier, inc=1, device_id={"row": y_peer(d)}, device_id_type=MESH)
    for d in range(1, C):
        pl.semaphore_signal(barrier, inc=1, device_id={"col": lax.rem(c + d, C)}, device_id_type=MESH)
    pl.semaphore_signal(barrier, inc=1, device_id={"layer": sib}, device_id_type=MESH)

    load_pattern = pltpu.make_async_copy(pattern_hbm, pattern_ref, load_sem.at[1])
    load_pattern.start()
    load_tile = pltpu.make_async_copy(density_ref, tile, load_sem.at[0])
    load_tile.start()
    load_panel = []
    for q in range(PIECES):
        at = pl.ds(pl.multiple_of(l * W + q * wq, wq), wq)
        load_panel.append(pltpu.make_async_copy(panel_ref.at[:, at], p.at[q, 0:tr, :], load_sem.at[2 + q]))
        load_panel[q].start()
    first, second = range(PIECES // 2), range(PIECES // 2, PIECES)

    def cols_of(col, extra=0, width=block):
        at = col * ti + extra
        row = at // tr
        dy, dx = lax.rem(y - row // A + B, B), lax.rem(x - lax.rem(row, A) + A, A)
        return pl.ds(pl.multiple_of((dy * A + dx) * tr + lax.rem(at, tr), width), width)

    def rows_of(slot):
        return slice(slot * tr, (slot + 1) * tr)

    own_half = pl.ds(pl.multiple_of(l * half, half), half)

    def column(slot):
        return fcol.at[rows_of(slot), own_half]

    def half_rows(slot, which):
        return fcol.at[slot * tr + which * hr:slot * tr + (which + 1) * hr, own_half]

    def half_of(layer):
        return pl.ds(pl.multiple_of(layer * hr, hr), hr)

    def row_tile(buf, col, layer, j):
        return buf.at[half_of(layer), cols_of(col, j * block)]

    def piece(slot, q):
        return p.at[q, rows_of(slot), :]

    def x_source(d):
        return y * A + lax.rem(x - d + A, A)

    def y_source(d):
        return lax.rem(y - d + B, B) * A + x

    sends = []

    def send(ref, ssem, rsem, dev, src=None):
        copy = pltpu.make_async_remote_copy(
            src_ref=ref if src is None else src, dst_ref=ref, send_sem=ssem, recv_sem=rsem,
            device_id=dev, device_id_type=MESH,
        )
        copy.start()
        sends.append(copy)

    def arrived(ref, ssem, rsem, dev):
        rem_copy(ref, ssem, rsem, dev).wait_recv()

    x_order = list(second) + list(first)
    y_order = list(first) + list(second)

    def send_own(n):
        qx, qy = x_order[n], y_order[n]
        for d in range(1, A):
            send(piece(d, qx), px_s.at[d, qx], px_r.at[d, qx], {"row": x_peer(d)}, piece(0, qx))
        for d in range(1, B):
            send(piece(d * A, qy), py_s.at[d, qy], py_r.at[d, qy], {"row": y_peer(d)}, piece(0, qy))

    load_pattern.wait()
    load_tile.wait()
    for a in range(tr // BS):
        for b in range(ti // BS):
            keep = pattern_ref[a, b].astype(jnp.float32)
            masked = tile[a * BS:(a + 1) * BS, b * BS:(b + 1) * BS].astype(jnp.float32) * keep
            frow[a * BS:(a + 1) * BS, cols_of(c, b * BS, BS)] = masked.astype(jnp.bfloat16)
    for j in blocks:
        fcol[rows_of(0), j * block:(j + 1) * block] = frow[:, cols_of(c, j * block)]

    pl.semaphore_wait(barrier, A - 1 + B - 1 + C - 1 + 1)
    for d in range(1, C):
        for j in blocks:
            send(row_tile(frow, c, l, j), fr_s.at[d, j], fr_r.at[d, j], {"col": lax.rem(c + d, C)})
    own_rows = column(0)
    for d in range(1, A):
        send(column(d), cx_s.at[d], cx_r.at[d], {"row": x_peer(d)}, own_rows)
    for d in range(1, B):
        send(column(d * A), cy_s.at[d], cy_r.at[d], {"row": y_peer(d)}, own_rows)
    for copy in load_panel:
        copy.wait()
    send_own(0)
    send_own(1)

    for dy in range(1, B):
        arrived(column(dy * A), cy_s.at[dy], cy_r.at[dy], {"row": y_source(dy)})
        send(column(dy * A), cs_s.at[dy * A], cs_r.at[dy * A], {"layer": sib})
        for dx in range(1, A):
            send(half_rows(dy * A + dx, 0), ex_s.at[dy, dx], ex_r.at[dy, dx], {"row": x_peer(dx)},
                 half_rows(dy * A, 0))
    for dx in range(1, A):
        arrived(column(dx), cx_s.at[dx], cx_r.at[dx], {"row": x_source(dx)})
        send(column(dx), cs_s.at[dx], cs_r.at[dx], {"layer": sib})
        for dy in range(1, B):
            send(half_rows(dy * A + dx, 1), ey_s.at[dy, dx], ey_r.at[dy, dx], {"row": y_peer(dy)},
                 half_rows(dx, 1))
    for n in range(2, PIECES - 1):
        send_own(n)

    for dy in range(1, B):
        for dx in range(1, A):
            slot = dy * A + dx
            arrived(half_rows(slot, 0), ex_s.at[dy, dx], ex_r.at[dy, dx], {"row": x_source(dx)})
            arrived(half_rows(slot, 1), ey_s.at[dy, dx], ey_r.at[dy, dx], {"row": y_source(dy)})
            send(column(slot), cs_s.at[slot], cs_r.at[slot], {"layer": sib})

    for d in range(1, C):
        from_c = lax.rem(c - d + C, C)
        for j in blocks:
            ref = row_tile(frow, from_c, l, j)
            arrived(ref, fr_s.at[d, j], fr_r.at[d, j], {"col": from_c})
            send(ref, fs_s.at[d, j], fs_r.at[d, j], {"layer": sib})
    send_own(PIECES - 1)
    other_half = pl.ds(pl.multiple_of(sib * half, half), half)
    for slot in range(1, R):
        arrived(fcol.at[rows_of(slot), other_half], cs_s.at[slot], cs_r.at[slot], {"layer": sib})

    for j in blocks:
        grow[half_of(l), cols_of(c, j * block)] = jnp.dot(
            frow[half_of(l), :], fcol[:, j * block:(j + 1) * block], preferred_element_type=jnp.float32
        ).astype(jnp.bfloat16)
        ref = row_tile(grow, c, l, j)
        for d in range(1, C):
            send(ref, gr_s.at[d, j], gr_r.at[d, j], {"col": lax.rem(c + d, C)})
        send(ref, gs_s.at[0, j], gs_r.at[0, j], {"layer": sib})

    def part(q):
        return slice(q * wq, (q + 1) * wq)

    def by(left, group, q, rows=slice(None)):
        at = slice(group[0] * tr, group[1] * tr)
        return jnp.dot(left[rows, at], p[q, at, :], preferred_element_type=jnp.float32)

    near = [(0, A)]
    for dy in range(1, B):
        if dy * A == near[-1][1]:
            near[-1] = (near[-1][0], dy * A + 1)
        else:
            near.append((dy * A, dy * A + 1))
    far = [(dy * A + 1, dy * A + A) for dy in range(1, B)]

    early = len(sends)
    for qf, qs in zip(first, second):
        for dy in range(1, B):
            arrived(piece(dy * A, qf), py_s.at[dy, qf], py_r.at[dy, qf], {"row": y_source(dy)})
            for dx in range(1, A):
                send(piece(dy * A + dx, qf), fx_s.at[dy, dx, qf], fx_r.at[dy, dx, qf],
                     {"row": x_peer(dx)}, piece(dy * A, qf))
        for dx in range(1, A):
            arrived(piece(dx, qs), px_s.at[dx, qs], px_r.at[dx, qs], {"row": x_source(dx)})
            for dy in range(1, B):
                send(piece(dy * A + dx, qs), fy_s.at[dy, dx, qs], fy_r.at[dy, dx, qs],
                     {"row": y_peer(dy)}, piece(dx, qs))
    late = len(sends)

    for d in range(1, C):
        from_c = lax.rem(c - d + C, C)
        for j in blocks:
            ref = row_tile(grow, from_c, l, j)
            arrived(ref, gr_s.at[d, j], gr_r.at[d, j], {"col": from_c})
            send(ref, gs_s.at[d, j], gs_r.at[d, j], {"layer": sib})
    for d in range(1, C):
        from_c = lax.rem(c - d + C, C)
        for j in blocks:
            arrived(row_tile(frow, from_c, sib, j), fs_s.at[d, j], fs_r.at[d, j], {"layer": sib})
    for qf, qs in zip(first, second):
        for dy in range(1, B):
            arrived(piece(dy * A, qs), py_s.at[dy, qs], py_r.at[dy, qs], {"row": y_source(dy)})
        for dx in range(1, A):
            arrived(piece(dx, qf), px_s.at[dx, qf], px_r.at[dx, qf], {"row": x_source(dx)})
        for q in (qf, qs):
            acc[:, part(q)] = 3.0 * sum(by(frow, group, q) for group in near)
    for q in range(PIECES):
        acc[half_of(l), part(q)] -= 2.0 * sum(by(grow, group, q, half_of(l)) for group in near)
    for d in range(C):
        from_c = lax.rem(c - d + C, C)
        for j in blocks:
            arrived(row_tile(grow, from_c, sib, j), gs_s.at[d, j], gs_r.at[d, j], {"layer": sib})
    for q in range(PIECES):
        acc[half_of(sib), part(q)] -= 2.0 * sum(by(grow, group, q, half_of(sib)) for group in near)

    for copy in sends[:early] + sends[late:]:
        copy.wait_send()
    for qf, qs in zip(first, second):
        for dy in range(1, B):
            for dx in range(1, A):
                slot = dy * A + dx
                arrived(piece(slot, qf), fx_s.at[dy, dx, qf], fx_r.at[dy, dx, qf], {"row": x_source(dx)})
                arrived(piece(slot, qs), fy_s.at[dy, dx, qs], fy_r.at[dy, dx, qs], {"row": y_source(dy)})
        for q in (qf, qs):
            total = acc[:, part(q)]
            for group in far:
                total = total + (3.0 * by(frow, group, q) - 2.0 * by(grow, group, q))
            out_ref[:, part(q)] = total.astype(jnp.bfloat16)

    for copy in sends[early:late]:
        copy.wait_send()


def shards(R, C, L, density, panel, pattern):
    A = 1
    while A * A < R:
        A *= 2
    B = R // A
    tr, ti = density.shape
    nb = max(ti // tr, 1)
    W = panel.shape[1] // L
    K = tr * R
    dma = pltpu.SemaphoreType.DMA
    any_spec = pl.BlockSpec(memory_space=pl.ANY)
    bf16 = jnp.bfloat16
    return pl.pallas_call(
        functools.partial(kernel, (R, A, C)),
        out_shape=pltpu.VMEM((tr, W), bf16),
        in_specs=[any_spec] * 3,
        out_specs=pl.BlockSpec(memory_space=pltpu.VMEM),
        scratch_shapes=[
            pltpu.SMEM(pattern.shape, jnp.int32),
            pltpu.VMEM((tr, ti), bf16),
            pltpu.VMEM((K, ti), bf16),
            pltpu.VMEM((tr, K), bf16),
            pltpu.VMEM((tr, K), bf16),
            pltpu.VMEM((PIECES, K, W // PIECES), bf16),
            pltpu.VMEM((tr, W), jnp.float32),
            dma((2 + PIECES,)),
            dma((A,)), dma((A,)), dma((B,)), dma((B,)),
            dma((B, A)), dma((B, A)), dma((B, A)), dma((B, A)),
            dma((R,)), dma((R,)),
            dma((C, nb)), dma((C, nb)), dma((C, nb)), dma((C, nb)),
            dma((C, nb)), dma((C, nb)), dma((C, nb)), dma((C, nb)),
            dma((A, PIECES)), dma((A, PIECES)),
            dma((B, PIECES)), dma((B, PIECES)),
            dma((B, A, PIECES)), dma((B, A, PIECES)),
            dma((B, A, PIECES)), dma((B, A, PIECES)),
        ],
        compiler_params=pltpu.CompilerParams(
            collective_id=0, has_side_effects=True, vmem_limit_bytes=56 * 1024 * 1024
        ),
    )(density, panel, pattern)


def solution(mesh):
    R, C, L = mesh.shape["row"], mesh.shape["col"], mesh.shape["layer"]
    in_specs = (P("row", "col"), P("row", "col"), P("row", "col"))
    out_specs = P("row", ("col", "layer"))
    return jax.shard_map(
        functools.partial(shards, R, C, L),
        mesh=mesh, in_specs=in_specs, out_specs=out_specs, check_vma=False,
    )
```

```python
import functools

import jax
import jax.numpy as jnp
from jax import lax
from jax.experimental import pallas as pl
from jax.experimental.pallas import tpu as pltpu
from jax.sharding import PartitionSpec as P

BS = 128
PIECES = 4
MESH = pl.DeviceIdType.MESH


def kernel(
    sizes, density_ref, panel_ref, pattern_hbm, out_ref,
    pattern_ref, tile, fcol, frow, grow, p, acc,
    go, load_sem, cx_s, cx_r, cy_s, cy_r, ex_s, ex_r, ey_s, ey_r, fr_s, fr_r, fs_s, fs_r, gr_s, gr_r, gs_s, gs_r,
    px_s, px_r, py_s, py_r, fx_s, fx_r, fy_s, fy_r,
):
    R, A, C = sizes
    B = R // A
    tr, ti = density_ref.shape
    half = ti // 2
    wq = p.shape[2]
    W = wq * PIECES
    r = lax.axis_index("row")
    c = lax.axis_index("col")
    l = lax.axis_index("layer")
    x = lax.rem(r, A)
    y = r // A
    sib = 1 - l

    def rem_copy(ref, ssem, rsem, dev):
        return pltpu.make_async_remote_copy(
            src_ref=ref, dst_ref=ref, send_sem=ssem, recv_sem=rsem,
            device_id=dev, device_id_type=MESH,
        )

    def x_peer(d):
        return y * A + lax.rem(x + d, A)

    def y_peer(d):
        return lax.rem(y + d, B) * A + x

    barrier = pltpu.get_barrier_semaphore()
    def greet(sem, peers):
        for peer in peers:
            pl.semaphore_signal(sem, inc=1, device_id=peer, device_id_type=MESH)

    row_peers = [{"row": x_peer(d)} for d in range(1, A)] + [{"row": y_peer(d)} for d in range(1, B)]
    col_peers = [{"col": lax.rem(c + d, C)} for d in range(1, C)]
    sibling = [{"layer": sib}]

    @pl.when(l == 0)
    def _():
        greet(barrier, row_peers + sibling)

    @pl.when(l == 1)
    def _():
        greet(barrier, col_peers + sibling)

    load_pattern = pltpu.make_async_copy(pattern_hbm, pattern_ref, load_sem.at[1])
    load_pattern.start()
    load_tile = pltpu.make_async_copy(density_ref, tile, load_sem.at[0])
    load_tile.start()
    load_panel = []
    for q in range(PIECES):
        at = pl.ds(pl.multiple_of(l * W + q * wq, wq), wq)
        load_panel.append(pltpu.make_async_copy(panel_ref.at[:, at], p.at[q, 0:tr, :], load_sem.at[2 + q]))
        load_panel[q].start()
    first, second = range(PIECES // 2), range(PIECES // 2, PIECES)

    def cols_of(col, layer, width=half, extra=0):
        at = col * ti + layer * half + extra
        row = at // tr
        dy, dx = lax.rem(y - row // A + B, B), lax.rem(x - lax.rem(row, A) + A, A)
        return pl.ds(pl.multiple_of((dy * A + dx) * tr + lax.rem(at, tr), width), width)

    def rows_of(slot):
        return slice(slot * tr, (slot + 1) * tr)

    def half_rows(slot, which):
        return fcol.at[slot * tr + which * (tr // 2):slot * tr + (which + 1) * (tr // 2), :]

    def piece(slot, q):
        return p.at[q, rows_of(slot), :]

    def x_source(d):
        return y * A + lax.rem(x - d + A, A)

    def y_source(d):
        return lax.rem(y - d + B, B) * A + x

    sends = []

    def prepare(ref, ssem, rsem, dev, src=None):
        copy = pltpu.make_async_remote_copy(
            src_ref=ref if src is None else src, dst_ref=ref, send_sem=ssem, recv_sem=rsem,
            device_id=dev, device_id_type=MESH,
        )
        sends.append(copy)
        return copy

    def send(*args):
        prepare(*args).start()

    def arrived(ref, ssem, rsem, dev):
        rem_copy(ref, ssem, rsem, dev).wait_recv()

    x_order = list(second) + list(first)
    y_order = list(first) + list(second)

    def own_piece(n):
        qx, qy = x_order[n], y_order[n]
        return [
            prepare(piece(d, qx), px_s.at[d, qx], px_r.at[d, qx], {"row": x_peer(d)}, piece(0, qx))
            for d in range(1, A)
        ] + [
            prepare(piece(d * A, qy), py_s.at[d, qy], py_r.at[d, qy], {"row": y_peer(d)}, piece(0, qy))
            for d in range(1, B)
        ]

    load_pattern.wait()
    load_tile.wait()
    for a in range(tr // BS):
        for b in range(ti // BS):
            keep = pattern_ref[a, b].astype(jnp.float32)
            block = tile[a * BS:(a + 1) * BS, b * BS:(b + 1) * BS].astype(jnp.float32) * keep
            frow[a * BS:(a + 1) * BS, cols_of(c, 0, BS, b * BS)] = block.astype(jnp.bfloat16)
    fcol[rows_of(0), :] = frow[:, cols_of(c, l)]

    own_rows = fcol.at[rows_of(0), :]
    over_col = [
        prepare(frow.at[:, cols_of(c, l)], fr_s.at[d], fr_r.at[d], {"col": lax.rem(c + d, C)})
        for d in range(1, C)
    ]
    over_row = [
        prepare(fcol.at[rows_of(d), :], cx_s.at[d], cx_r.at[d], {"row": x_peer(d)}, own_rows)
        for d in range(1, A)
    ] + [
        prepare(fcol.at[rows_of(d * A), :], cy_s.at[d], cy_r.at[d], {"row": y_peer(d)}, own_rows)
        for d in range(1, B)
    ]
    for n in range(PIECES):
        over_row += own_piece(n)
    for copy in load_panel:
        copy.wait()

    @pl.when(l == 0)
    def _():
        pl.semaphore_wait(barrier, len(row_peers) + 1)
        greet(go.at[0], row_peers)
        for copy in over_row:
            copy.start()
        pl.semaphore_wait(go.at[0], len(row_peers))
        greet(go.at[2], sibling)
        pl.semaphore_wait(go.at[2], 1)
        for copy in over_col:
            copy.start()

    @pl.when(l == 1)
    def _():
        pl.semaphore_wait(barrier, len(col_peers) + 1)
        greet(go.at[1], col_peers)
        for copy in over_col:
            copy.start()
        pl.semaphore_wait(go.at[1], len(col_peers))
        greet(go.at[2], sibling)
        pl.semaphore_wait(go.at[2], 1)
        for copy in over_row:
            copy.start()

    for dy in range(1, B):
        arrived(fcol.at[rows_of(dy * A), :], cy_s.at[dy], cy_r.at[dy], {"row": y_source(dy)})
        for dx in range(1, A):
            send(half_rows(dy * A + dx, 0), ex_s.at[dy, dx], ex_r.at[dy, dx], {"row": x_peer(dx)},
                 half_rows(dy * A, 0))
    for dx in range(1, A):
        arrived(fcol.at[rows_of(dx), :], cx_s.at[dx], cx_r.at[dx], {"row": x_source(dx)})
        for dy in range(1, B):
            send(half_rows(dy * A + dx, 1), ey_s.at[dy, dx], ey_r.at[dy, dx], {"row": y_peer(dy)},
                 half_rows(dx, 1))

    for d in range(1, C):
        from_c = lax.rem(c - d + C, C)
        ref = frow.at[:, cols_of(from_c, l)]
        arrived(ref, fr_s.at[d], fr_r.at[d], {"col": from_c})
        send(ref, fs_s.at[d], fs_r.at[d], {"layer": sib})
    for d in range(1, C):
        from_c = lax.rem(c - d + C, C)
        arrived(frow.at[:, cols_of(from_c, sib)], fs_s.at[d], fs_r.at[d], {"layer": sib})
    for dy in range(1, B):
        for dx in range(1, A):
            slot = dy * A + dx
            arrived(half_rows(slot, 0), ex_s.at[dy, dx], ex_r.at[dy, dx], {"row": x_source(dx)})
            arrived(half_rows(slot, 1), ey_s.at[dy, dx], ey_r.at[dy, dx], {"row": y_source(dy)})

    grow[:, cols_of(c, l)] = jnp.dot(
        frow[...], fcol[...], preferred_element_type=jnp.float32
    ).astype(jnp.bfloat16)
    for d in range(1, C):
        send(grow.at[:, cols_of(c, l)], gr_s.at[d], gr_r.at[d], {"col": lax.rem(c + d, C)})
    send(grow.at[:, cols_of(c, l)], gs_s.at[0], gs_r.at[0], {"layer": sib})

    def part(q):
        return slice(q * wq, (q + 1) * wq)

    def by(left, group, q):
        at = slice(group[0] * tr, group[1] * tr)
        return jnp.dot(left[:, at], p[q, at, :], preferred_element_type=jnp.float32)

    near = [(0, A)]
    for dy in range(1, B):
        if dy * A == near[-1][1]:
            near[-1] = (near[-1][0], dy * A + 1)
        else:
            near.append((dy * A, dy * A + 1))
    far = [(dy * A + 1, dy * A + A) for dy in range(1, B)]

    early = len(sends)
    for qf, qs in zip(first, second):
        for dy in range(1, B):
            arrived(piece(dy * A, qf), py_s.at[dy, qf], py_r.at[dy, qf], {"row": y_source(dy)})
            for dx in range(1, A):
                send(piece(dy * A + dx, qf), fx_s.at[dy, dx, qf], fx_r.at[dy, dx, qf],
                     {"row": x_peer(dx)}, piece(dy * A, qf))
        for dx in range(1, A):
            arrived(piece(dx, qs), px_s.at[dx, qs], px_r.at[dx, qs], {"row": x_source(dx)})
            for dy in range(1, B):
                send(piece(dy * A + dx, qs), fy_s.at[dy, dx, qs], fy_r.at[dy, dx, qs],
                     {"row": y_peer(dy)}, piece(dx, qs))
    late = len(sends)

    for d in range(1, C):
        from_c = lax.rem(c - d + C, C)
        ref = grow.at[:, cols_of(from_c, l)]
        arrived(ref, gr_s.at[d], gr_r.at[d], {"col": from_c})
        send(ref, gs_s.at[d], gs_r.at[d], {"layer": sib})
    for qf, qs in zip(first, second):
        for dy in range(1, B):
            arrived(piece(dy * A, qs), py_s.at[dy, qs], py_r.at[dy, qs], {"row": y_source(dy)})
        for dx in range(1, A):
            arrived(piece(dx, qf), px_s.at[dx, qf], px_r.at[dx, qf], {"row": x_source(dx)})
        for q in (qf, qs):
            acc[:, part(q)] = 3.0 * sum(by(frow, group, q) for group in near)
    for d in range(C):
        from_c = lax.rem(c - d + C, C)
        arrived(grow.at[:, cols_of(from_c, sib)], gs_s.at[d], gs_r.at[d], {"layer": sib})
    for q in range(PIECES):
        acc[:, part(q)] -= 2.0 * sum(by(grow, group, q) for group in near)

    for copy in sends[:early] + sends[late:]:
        copy.wait_send()
    for qf, qs in zip(first, second):
        for dy in range(1, B):
            for dx in range(1, A):
                slot = dy * A + dx
                arrived(piece(slot, qf), fx_s.at[dy, dx, qf], fx_r.at[dy, dx, qf], {"row": x_source(dx)})
                arrived(piece(slot, qs), fy_s.at[dy, dx, qs], fy_r.at[dy, dx, qs], {"row": y_source(dy)})
        for q in (qf, qs):
            total = acc[:, part(q)]
            for group in far:
                total = total + (3.0 * by(frow, group, q) - 2.0 * by(grow, group, q))
            out_ref[:, part(q)] = total.astype(jnp.bfloat16)

    for copy in sends[early:late]:
        copy.wait_send()


def shards(R, C, L, density, panel, pattern):
    A = 1
    while A * A < R:
        A *= 2
    B = R // A
    tr, ti = density.shape
    half = ti // L
    W = panel.shape[1] // L
    K = tr * R
    dma = pltpu.SemaphoreType.DMA
    any_spec = pl.BlockSpec(memory_space=pl.ANY)
    bf16 = jnp.bfloat16
    return pl.pallas_call(
        functools.partial(kernel, (R, A, C)),
        out_shape=pltpu.VMEM((tr, W), bf16),
        in_specs=[any_spec] * 3,
        out_specs=pl.BlockSpec(memory_space=pltpu.VMEM),
        scratch_shapes=[
            pltpu.SMEM(pattern.shape, jnp.int32),
            pltpu.VMEM((tr, ti), bf16),
            pltpu.VMEM((K, half), bf16),
            pltpu.VMEM((tr, K), bf16),
            pltpu.VMEM((tr, K), bf16),
            pltpu.VMEM((PIECES, K, W // PIECES), bf16),
            pltpu.VMEM((tr, W), jnp.float32),
            pltpu.SemaphoreType.REGULAR((3,)),
            dma((2 + PIECES,)),
            dma((A,)), dma((A,)), dma((B,)), dma((B,)),
            dma((B, A)), dma((B, A)), dma((B, A)), dma((B, A)),
            dma((C,)), dma((C,)), dma((C,)), dma((C,)),
            dma((C,)), dma((C,)), dma((C,)), dma((C,)),
            dma((A, PIECES)), dma((A, PIECES)),
            dma((B, PIECES)), dma((B, PIECES)),
            dma((B, A, PIECES)), dma((B, A, PIECES)),
            dma((B, A, PIECES)), dma((B, A, PIECES)),
        ],
        compiler_params=pltpu.CompilerParams(
            collective_id=0, has_side_effects=True, vmem_limit_bytes=56 * 1024 * 1024
        ),
    )(density, panel, pattern)


def solution(mesh):
    R, C, L = mesh.shape["row"], mesh.shape["col"], mesh.shape["layer"]
    in_specs = (P("row", "col"), P("row", "col"), P("row", "col"))
    out_specs = P("row", ("col", "layer"))
    return jax.shard_map(
        functools.partial(shards, R, C, L),
        mesh=mesh, in_specs=in_specs, out_specs=out_specs, check_vma=False,
    )
```

```python
import functools

import jax
import jax.numpy as jnp
from jax import lax
from jax.experimental import pallas as pl
from jax.experimental.pallas import tpu as pltpu
from jax.sharding import PartitionSpec as P

BS = 128
PIECES = 4
MESH = pl.DeviceIdType.MESH


def kernel(
    sizes, density_ref, panel_ref, pattern_hbm, out_ref,
    pattern_ref, tile, fcol, frow, grow, p, acc,
    go, load_sem, cx_s, cx_r, cy_s, cy_r, ex_s, ex_r, ey_s, ey_r, fr_s, fr_r, fs_s, fs_r, gr_s, gr_r, gs_s, gs_r,
    px_s, px_r, py_s, py_r, fx_s, fx_r, fy_s, fy_r,
):
    R, A, C = sizes
    B = R // A
    tr, ti = density_ref.shape
    half = ti // 2
    wq = p.shape[2]
    W = wq * PIECES
    r = lax.axis_index("row")
    c = lax.axis_index("col")
    l = lax.axis_index("layer")
    x = lax.rem(r, A)
    y = r // A
    sib = 1 - l

    def rem_copy(ref, ssem, rsem, dev):
        return pltpu.make_async_remote_copy(
            src_ref=ref, dst_ref=ref, send_sem=ssem, recv_sem=rsem,
            device_id=dev, device_id_type=MESH,
        )

    def x_peer(d):
        return y * A + lax.rem(x + d, A)

    def y_peer(d):
        return lax.rem(y + d, B) * A + x

    barrier = pltpu.get_barrier_semaphore()
    def greet(sem, peers):
        for peer in peers:
            pl.semaphore_signal(sem, inc=1, device_id=peer, device_id_type=MESH)

    row_peers = [{"row": x_peer(d)} for d in range(1, A)] + [{"row": y_peer(d)} for d in range(1, B)]
    col_peers = [{"col": lax.rem(c + d, C)} for d in range(1, C)]
    sibling = [{"layer": sib}]

    @pl.when(l == 0)
    def _():
        greet(barrier, row_peers + sibling)

    @pl.when(l == 1)
    def _():
        greet(barrier, col_peers + sibling)

    load_pattern = pltpu.make_async_copy(pattern_hbm, pattern_ref, load_sem.at[1])
    load_pattern.start()
    load_tile = pltpu.make_async_copy(density_ref, tile, load_sem.at[0])
    load_tile.start()
    load_panel = []
    for q in range(PIECES):
        at = pl.ds(pl.multiple_of(l * W + q * wq, wq), wq)
        load_panel.append(pltpu.make_async_copy(panel_ref.at[:, at], p.at[q, 0:tr, :], load_sem.at[2 + q]))
        load_panel[q].start()
    first, second = range(PIECES // 2), range(PIECES // 2, PIECES)

    def cols_of(col, layer, width=half, extra=0):
        at = col * ti + layer * half + extra
        row = at // tr
        dy, dx = lax.rem(y - row // A + B, B), lax.rem(x - lax.rem(row, A) + A, A)
        return pl.ds(pl.multiple_of((dy * A + dx) * tr + lax.rem(at, tr), width), width)

    def rows_of(slot):
        return slice(slot * tr, (slot + 1) * tr)

    def half_rows(slot, which):
        return fcol.at[slot * tr + which * (tr // 2):slot * tr + (which + 1) * (tr // 2), :]

    def piece(slot, q):
        return p.at[q, rows_of(slot), :]

    def x_source(d):
        return y * A + lax.rem(x - d + A, A)

    def y_source(d):
        return lax.rem(y - d + B, B) * A + x

    sends = []

    def prepare(ref, ssem, rsem, dev, src=None):
        copy = pltpu.make_async_remote_copy(
            src_ref=ref if src is None else src, dst_ref=ref, send_sem=ssem, recv_sem=rsem,
            device_id=dev, device_id_type=MESH,
        )
        sends.append(copy)
        return copy

    def send(*args):
        prepare(*args).start()

    def arrived(ref, ssem, rsem, dev):
        rem_copy(ref, ssem, rsem, dev).wait_recv()

    x_order = list(second) + list(first)
    y_order = list(first) + list(second)

    def own_piece(n):
        qx, qy = x_order[n], y_order[n]
        return [
            prepare(piece(d, qx), px_s.at[d, qx], px_r.at[d, qx], {"row": x_peer(d)}, piece(0, qx))
            for d in range(1, A)
        ] + [
            prepare(piece(d * A, qy), py_s.at[d, qy], py_r.at[d, qy], {"row": y_peer(d)}, piece(0, qy))
            for d in range(1, B)
        ]

    load_pattern.wait()
    load_tile.wait()
    for a in range(tr // BS):
        for b in range(ti // BS):
            keep = pattern_ref[a, b].astype(jnp.float32)
            block = tile[a * BS:(a + 1) * BS, b * BS:(b + 1) * BS].astype(jnp.float32) * keep
            frow[a * BS:(a + 1) * BS, cols_of(c, 0, BS, b * BS)] = block.astype(jnp.bfloat16)
    fcol[rows_of(0), :] = frow[:, cols_of(c, l)]

    own_rows = fcol.at[rows_of(0), :]
    over_col = [
        prepare(frow.at[:, cols_of(c, l)], fr_s.at[d], fr_r.at[d], {"col": lax.rem(c + d, C)})
        for d in range(1, C)
    ]
    over_row = [
        prepare(fcol.at[rows_of(d), :], cx_s.at[d], cx_r.at[d], {"row": x_peer(d)}, own_rows)
        for d in range(1, A)
    ] + [
        prepare(fcol.at[rows_of(d * A), :], cy_s.at[d], cy_r.at[d], {"row": y_peer(d)}, own_rows)
        for d in range(1, B)
    ]
    for n in range(2):
        over_row += own_piece(n)
    for copy in load_panel:
        copy.wait()

    @pl.when(l == 0)
    def _():
        pl.semaphore_wait(barrier, len(row_peers) + 1)
        greet(go.at[0], row_peers)
        for copy in over_row:
            copy.start()
        pl.semaphore_wait(go.at[0], len(row_peers))
        greet(go.at[2], sibling)
        pl.semaphore_wait(go.at[2], 1)
        for copy in over_col:
            copy.start()

    @pl.when(l == 1)
    def _():
        pl.semaphore_wait(barrier, len(col_peers) + 1)
        greet(go.at[1], col_peers)
        for copy in over_col:
            copy.start()
        pl.semaphore_wait(go.at[1], len(col_peers))
        greet(go.at[2], sibling)
        pl.semaphore_wait(go.at[2], 1)
        for copy in over_row:
            copy.start()

    for dy in range(1, B):
        arrived(fcol.at[rows_of(dy * A), :], cy_s.at[dy], cy_r.at[dy], {"row": y_source(dy)})
        for dx in range(1, A):
            send(half_rows(dy * A + dx, 0), ex_s.at[dy, dx], ex_r.at[dy, dx], {"row": x_peer(dx)},
                 half_rows(dy * A, 0))
    for dx in range(1, A):
        arrived(fcol.at[rows_of(dx), :], cx_s.at[dx], cx_r.at[dx], {"row": x_source(dx)})
        for dy in range(1, B):
            send(half_rows(dy * A + dx, 1), ey_s.at[dy, dx], ey_r.at[dy, dx], {"row": y_peer(dy)},
                 half_rows(dx, 1))

    for n in range(2, PIECES):
        for copy in own_piece(n):
            copy.start()

    for d in range(1, C):
        from_c = lax.rem(c - d + C, C)
        ref = frow.at[:, cols_of(from_c, l)]
        arrived(ref, fr_s.at[d], fr_r.at[d], {"col": from_c})
        send(ref, fs_s.at[d], fs_r.at[d], {"layer": sib})
    for d in range(1, C):
        from_c = lax.rem(c - d + C, C)
        arrived(frow.at[:, cols_of(from_c, sib)], fs_s.at[d], fs_r.at[d], {"layer": sib})
    for dy in range(1, B):
        for dx in range(1, A):
            slot = dy * A + dx
            arrived(half_rows(slot, 0), ex_s.at[dy, dx], ex_r.at[dy, dx], {"row": x_source(dx)})
            arrived(half_rows(slot, 1), ey_s.at[dy, dx], ey_r.at[dy, dx], {"row": y_source(dy)})

    grow[:, cols_of(c, l)] = jnp.dot(
        frow[...], fcol[...], preferred_element_type=jnp.float32
    ).astype(jnp.bfloat16)
    for d in range(1, C):
        send(grow.at[:, cols_of(c, l)], gr_s.at[d], gr_r.at[d], {"col": lax.rem(c + d, C)})
    send(grow.at[:, cols_of(c, l)], gs_s.at[0], gs_r.at[0], {"layer": sib})

    def part(q):
        return slice(q * wq, (q + 1) * wq)

    def by(left, group, q):
        at = slice(group[0] * tr, group[1] * tr)
        return jnp.dot(left[:, at], p[q, at, :], preferred_element_type=jnp.float32)

    near = [(0, A)]
    for dy in range(1, B):
        if dy * A == near[-1][1]:
            near[-1] = (near[-1][0], dy * A + 1)
        else:
            near.append((dy * A, dy * A + 1))
    far = [(dy * A + 1, dy * A + A) for dy in range(1, B)]

    early = len(sends)
    for qf, qs in zip(first, second):
        for dy in range(1, B):
            arrived(piece(dy * A, qf), py_s.at[dy, qf], py_r.at[dy, qf], {"row": y_source(dy)})
            for dx in range(1, A):
                send(piece(dy * A + dx, qf), fx_s.at[dy, dx, qf], fx_r.at[dy, dx, qf],
                     {"row": x_peer(dx)}, piece(dy * A, qf))
        for dx in range(1, A):
            arrived(piece(dx, qs), px_s.at[dx, qs], px_r.at[dx, qs], {"row": x_source(dx)})
            for dy in range(1, B):
                send(piece(dy * A + dx, qs), fy_s.at[dy, dx, qs], fy_r.at[dy, dx, qs],
                     {"row": y_peer(dy)}, piece(dx, qs))
    late = len(sends)

    for d in range(1, C):
        from_c = lax.rem(c - d + C, C)
        ref = grow.at[:, cols_of(from_c, l)]
        arrived(ref, gr_s.at[d], gr_r.at[d], {"col": from_c})
        send(ref, gs_s.at[d], gs_r.at[d], {"layer": sib})
    for qf, qs in zip(first, second):
        for dy in range(1, B):
            arrived(piece(dy * A, qs), py_s.at[dy, qs], py_r.at[dy, qs], {"row": y_source(dy)})
        for dx in range(1, A):
            arrived(piece(dx, qf), px_s.at[dx, qf], px_r.at[dx, qf], {"row": x_source(dx)})
        for q in (qf, qs):
            acc[:, part(q)] = 3.0 * sum(by(frow, group, q) for group in near)
    for d in range(C):
        from_c = lax.rem(c - d + C, C)
        arrived(grow.at[:, cols_of(from_c, sib)], gs_s.at[d], gs_r.at[d], {"layer": sib})
    for q in range(PIECES):
        acc[:, part(q)] -= 2.0 * sum(by(grow, group, q) for group in near)

    for copy in sends[:early] + sends[late:]:
        copy.wait_send()
    for qf, qs in zip(first, second):
        for dy in range(1, B):
            for dx in range(1, A):
                slot = dy * A + dx
                arrived(piece(slot, qf), fx_s.at[dy, dx, qf], fx_r.at[dy, dx, qf], {"row": x_source(dx)})
                arrived(piece(slot, qs), fy_s.at[dy, dx, qs], fy_r.at[dy, dx, qs], {"row": y_source(dy)})
        for q in (qf, qs):
            total = acc[:, part(q)]
            for group in far:
                total = total + (3.0 * by(frow, group, q) - 2.0 * by(grow, group, q))
            out_ref[:, part(q)] = total.astype(jnp.bfloat16)

    for copy in sends[early:late]:
        copy.wait_send()


def shards(R, C, L, density, panel, pattern):
    A = 1
    while A * A < R:
        A *= 2
    B = R // A
    tr, ti = density.shape
    half = ti // L
    W = panel.shape[1] // L
    K = tr * R
    dma = pltpu.SemaphoreType.DMA
    any_spec = pl.BlockSpec(memory_space=pl.ANY)
    bf16 = jnp.bfloat16
    return pl.pallas_call(
        functools.partial(kernel, (R, A, C)),
        out_shape=pltpu.VMEM((tr, W), bf16),
        in_specs=[any_spec] * 3,
        out_specs=pl.BlockSpec(memory_space=pltpu.VMEM),
        scratch_shapes=[
            pltpu.SMEM(pattern.shape, jnp.int32),
            pltpu.VMEM((tr, ti), bf16),
            pltpu.VMEM((K, half), bf16),
            pltpu.VMEM((tr, K), bf16),
            pltpu.VMEM((tr, K), bf16),
            pltpu.VMEM((PIECES, K, W // PIECES), bf16),
            pltpu.VMEM((tr, W), jnp.float32),
            pltpu.SemaphoreType.REGULAR((3,)),
            dma((2 + PIECES,)),
            dma((A,)), dma((A,)), dma((B,)), dma((B,)),
            dma((B, A)), dma((B, A)), dma((B, A)), dma((B, A)),
            dma((C,)), dma((C,)), dma((C,)), dma((C,)),
            dma((C,)), dma((C,)), dma((C,)), dma((C,)),
            dma((A, PIECES)), dma((A, PIECES)),
            dma((B, PIECES)), dma((B, PIECES)),
            dma((B, A, PIECES)), dma((B, A, PIECES)),
            dma((B, A, PIECES)), dma((B, A, PIECES)),
        ],
        compiler_params=pltpu.CompilerParams(
            collective_id=0, has_side_effects=True, vmem_limit_bytes=56 * 1024 * 1024
        ),
    )(density, panel, pattern)


def solution(mesh):
    R, C, L = mesh.shape["row"], mesh.shape["col"], mesh.shape["layer"]
    in_specs = (P("row", "col"), P("row", "col"), P("row", "col"))
    out_specs = P("row", ("col", "layer"))
    return jax.shard_map(
        functools.partial(shards, R, C, L),
        mesh=mesh, in_specs=in_specs, out_specs=out_specs, check_vma=False,
    )
```

```python
import functools

import jax
import jax.numpy as jnp
from jax import lax
from jax.experimental import pallas as pl
from jax.experimental.pallas import tpu as pltpu
from jax.sharding import PartitionSpec as P

BS = 128
PIECES = 4
MESH = pl.DeviceIdType.MESH


def kernel(
    sizes, density_ref, panel_ref, pattern_hbm, out_ref,
    pattern_ref, tile, fcol, frow, grow, p, acc,
    go, load_sem, cx_s, cx_r, cy_s, cy_r, ex_s, ex_r, ey_s, ey_r, fr_s, fr_r, fs_s, fs_r, gr_s, gr_r, gs_s, gs_r,
    px_s, px_r, py_s, py_r, fx_s, fx_r, fy_s, fy_r,
):
    R, A, C = sizes
    B = R // A
    tr, ti = density_ref.shape
    half = ti // 2
    wq = p.shape[2]
    W = wq * PIECES
    r = lax.axis_index("row")
    c = lax.axis_index("col")
    l = lax.axis_index("layer")
    x = lax.rem(r, A)
    y = r // A
    sib = 1 - l

    def rem_copy(ref, ssem, rsem, dev):
        return pltpu.make_async_remote_copy(
            src_ref=ref, dst_ref=ref, send_sem=ssem, recv_sem=rsem,
            device_id=dev, device_id_type=MESH,
        )

    def x_peer(d):
        return y * A + lax.rem(x + d, A)

    def y_peer(d):
        return lax.rem(y + d, B) * A + x

    barrier = pltpu.get_barrier_semaphore()
    def greet(sem, peers):
        for peer in peers:
            pl.semaphore_signal(sem, inc=1, device_id=peer, device_id_type=MESH)

    row_peers = [{"row": x_peer(d)} for d in range(1, A)] + [{"row": y_peer(d)} for d in range(1, B)]
    col_peers = [{"col": lax.rem(c + d, C)} for d in range(1, C)]
    sibling = [{"layer": sib}]

    @pl.when(l == 0)
    def _():
        greet(barrier, row_peers + sibling)

    @pl.when(l == 1)
    def _():
        greet(barrier, col_peers + sibling)

    load_pattern = pltpu.make_async_copy(pattern_hbm, pattern_ref, load_sem.at[1])
    load_pattern.start()
    load_tile = pltpu.make_async_copy(density_ref, tile, load_sem.at[0])
    load_tile.start()
    load_panel = []
    for q in range(PIECES):
        at = pl.ds(pl.multiple_of(l * W + q * wq, wq), wq)
        load_panel.append(pltpu.make_async_copy(panel_ref.at[:, at], p.at[q, 0:tr, :], load_sem.at[2 + q]))
        load_panel[q].start()
    first, second = range(PIECES // 2), range(PIECES // 2, PIECES)

    def cols_of(col, layer, width=half, extra=0):
        at = col * ti + layer * half + extra
        row = at // tr
        dy, dx = lax.rem(y - row // A + B, B), lax.rem(x - lax.rem(row, A) + A, A)
        return pl.ds(pl.multiple_of((dy * A + dx) * tr + lax.rem(at, tr), width), width)

    def rows_of(slot):
        return slice(slot * tr, (slot + 1) * tr)

    def half_rows(slot, which):
        return fcol.at[slot * tr + which * (tr // 2):slot * tr + (which + 1) * (tr // 2), :]

    def piece(slot, q):
        return p.at[q, rows_of(slot), :]

    def x_source(d):
        return y * A + lax.rem(x - d + A, A)

    def y_source(d):
        return lax.rem(y - d + B, B) * A + x

    sends = []

    def prepare(ref, ssem, rsem, dev, src=None):
        copy = pltpu.make_async_remote_copy(
            src_ref=ref if src is None else src, dst_ref=ref, send_sem=ssem, recv_sem=rsem,
            device_id=dev, device_id_type=MESH,
        )
        sends.append(copy)
        return copy

    def send(*args):
        prepare(*args).start()

    def arrived(ref, ssem, rsem, dev):
        rem_copy(ref, ssem, rsem, dev).wait_recv()

    x_order = list(second) + list(first)
    y_order = list(first) + list(second)

    def own_piece(n):
        qx, qy = x_order[n], y_order[n]
        return [
            prepare(piece(d, qx), px_s.at[d, qx], px_r.at[d, qx], {"row": x_peer(d)}, piece(0, qx))
            for d in range(1, A)
        ] + [
            prepare(piece(d * A, qy), py_s.at[d, qy], py_r.at[d, qy], {"row": y_peer(d)}, piece(0, qy))
            for d in range(1, B)
        ]

    load_pattern.wait()
    load_tile.wait()
    for a in range(tr // BS):
        for b in range(ti // BS):
            keep = pattern_ref[a, b].astype(jnp.float32)
            block = tile[a * BS:(a + 1) * BS, b * BS:(b + 1) * BS].astype(jnp.float32) * keep
            frow[a * BS:(a + 1) * BS, cols_of(c, 0, BS, b * BS)] = block.astype(jnp.bfloat16)
    fcol[rows_of(0), :] = frow[:, cols_of(c, l)]

    own_rows = fcol.at[rows_of(0), :]
    over_col = [
        prepare(frow.at[:, cols_of(c, l)], fr_s.at[d], fr_r.at[d], {"col": lax.rem(c + d, C)})
        for d in range(1, C)
    ]
    over_row = [
        prepare(fcol.at[rows_of(d), :], cx_s.at[d], cx_r.at[d], {"row": x_peer(d)}, own_rows)
        for d in range(1, A)
    ] + [
        prepare(fcol.at[rows_of(d * A), :], cy_s.at[d], cy_r.at[d], {"row": y_peer(d)}, own_rows)
        for d in range(1, B)
    ]
    for n in range(2):
        over_row += own_piece(n)
    for copy in load_panel:
        copy.wait()

    @pl.when(l == 0)
    def _():
        pl.semaphore_wait(barrier, len(row_peers) + 1)
        greet(go.at[0], row_peers)
        for copy in over_row:
            copy.start()
        pl.semaphore_wait(go.at[0], len(row_peers))
        greet(go.at[2], sibling)
        pl.semaphore_wait(go.at[2], 1)
        for copy in over_col:
            copy.start()

    @pl.when(l == 1)
    def _():
        pl.semaphore_wait(go.at[2], 1)
        for copy in over_row:
            copy.start()
        pl.semaphore_wait(barrier, len(col_peers) + 1)
        greet(go.at[1], col_peers)
        for copy in over_col:
            copy.start()
        pl.semaphore_wait(go.at[1], len(col_peers))
        greet(go.at[2], sibling)

    for dy in range(1, B):
        arrived(fcol.at[rows_of(dy * A), :], cy_s.at[dy], cy_r.at[dy], {"row": y_source(dy)})
        for dx in range(1, A):
            send(half_rows(dy * A + dx, 0), ex_s.at[dy, dx], ex_r.at[dy, dx], {"row": x_peer(dx)},
                 half_rows(dy * A, 0))
    for dx in range(1, A):
        arrived(fcol.at[rows_of(dx), :], cx_s.at[dx], cx_r.at[dx], {"row": x_source(dx)})
        for dy in range(1, B):
            send(half_rows(dy * A + dx, 1), ey_s.at[dy, dx], ey_r.at[dy, dx], {"row": y_peer(dy)},
                 half_rows(dx, 1))

    for n in range(2, PIECES):
        for copy in own_piece(n):
            copy.start()

    for d in range(1, C):
        from_c = lax.rem(c - d + C, C)
        ref = frow.at[:, cols_of(from_c, l)]
        arrived(ref, fr_s.at[d], fr_r.at[d], {"col": from_c})
        send(ref, fs_s.at[d], fs_r.at[d], {"layer": sib})
    for d in range(1, C):
        from_c = lax.rem(c - d + C, C)
        arrived(frow.at[:, cols_of(from_c, sib)], fs_s.at[d], fs_r.at[d], {"layer": sib})
    for dy in range(1, B):
        for dx in range(1, A):
            slot = dy * A + dx
            arrived(half_rows(slot, 0), ex_s.at[dy, dx], ex_r.at[dy, dx], {"row": x_source(dx)})
            arrived(half_rows(slot, 1), ey_s.at[dy, dx], ey_r.at[dy, dx], {"row": y_source(dy)})

    grow[:, cols_of(c, l)] = jnp.dot(
        frow[...], fcol[...], preferred_element_type=jnp.float32
    ).astype(jnp.bfloat16)
    for d in range(1, C):
        send(grow.at[:, cols_of(c, l)], gr_s.at[d], gr_r.at[d], {"col": lax.rem(c + d, C)})
    send(grow.at[:, cols_of(c, l)], gs_s.at[0], gs_r.at[0], {"layer": sib})

    def part(q):
        return slice(q * wq, (q + 1) * wq)

    def by(left, group, q):
        at = slice(group[0] * tr, group[1] * tr)
        return jnp.dot(left[:, at], p[q, at, :], preferred_element_type=jnp.float32)

    near = [(0, A)]
    for dy in range(1, B):
        if dy * A == near[-1][1]:
            near[-1] = (near[-1][0], dy * A + 1)
        else:
            near.append((dy * A, dy * A + 1))
    far = [(dy * A + 1, dy * A + A) for dy in range(1, B)]

    early = len(sends)
    for qf, qs in zip(first, second):
        for dy in range(1, B):
            arrived(piece(dy * A, qf), py_s.at[dy, qf], py_r.at[dy, qf], {"row": y_source(dy)})
            for dx in range(1, A):
                send(piece(dy * A + dx, qf), fx_s.at[dy, dx, qf], fx_r.at[dy, dx, qf],
                     {"row": x_peer(dx)}, piece(dy * A, qf))
        for dx in range(1, A):
            arrived(piece(dx, qs), px_s.at[dx, qs], px_r.at[dx, qs], {"row": x_source(dx)})
            for dy in range(1, B):
                send(piece(dy * A + dx, qs), fy_s.at[dy, dx, qs], fy_r.at[dy, dx, qs],
                     {"row": y_peer(dy)}, piece(dx, qs))
    late = len(sends)

    for d in range(1, C):
        from_c = lax.rem(c - d + C, C)
        ref = grow.at[:, cols_of(from_c, l)]
        arrived(ref, gr_s.at[d], gr_r.at[d], {"col": from_c})
        send(ref, gs_s.at[d], gs_r.at[d], {"layer": sib})
    for qf, qs in zip(first, second):
        for dy in range(1, B):
            arrived(piece(dy * A, qs), py_s.at[dy, qs], py_r.at[dy, qs], {"row": y_source(dy)})
        for dx in range(1, A):
            arrived(piece(dx, qf), px_s.at[dx, qf], px_r.at[dx, qf], {"row": x_source(dx)})
        for q in (qf, qs):
            acc[:, part(q)] = 3.0 * sum(by(frow, group, q) for group in near)
    for d in range(C):
        from_c = lax.rem(c - d + C, C)
        arrived(grow.at[:, cols_of(from_c, sib)], gs_s.at[d], gs_r.at[d], {"layer": sib})
    for q in range(PIECES):
        acc[:, part(q)] -= 2.0 * sum(by(grow, group, q) for group in near)

    for copy in sends[:early] + sends[late:]:
        copy.wait_send()
    for qf, qs in zip(first, second):
        for dy in range(1, B):
            for dx in range(1, A):
                slot = dy * A + dx
                arrived(piece(slot, qf), fx_s.at[dy, dx, qf], fx_r.at[dy, dx, qf], {"row": x_source(dx)})
                arrived(piece(slot, qs), fy_s.at[dy, dx, qs], fy_r.at[dy, dx, qs], {"row": y_source(dy)})
        for q in (qf, qs):
            total = acc[:, part(q)]
            for group in far:
                total = total + (3.0 * by(frow, group, q) - 2.0 * by(grow, group, q))
            out_ref[:, part(q)] = total.astype(jnp.bfloat16)

    for copy in sends[early:late]:
        copy.wait_send()


def shards(R, C, L, density, panel, pattern):
    A = 1
    while A * A < R:
        A *= 2
    B = R // A
    tr, ti = density.shape
    half = ti // L
    W = panel.shape[1] // L
    K = tr * R
    dma = pltpu.SemaphoreType.DMA
    any_spec = pl.BlockSpec(memory_space=pl.ANY)
    bf16 = jnp.bfloat16
    return pl.pallas_call(
        functools.partial(kernel, (R, A, C)),
        out_shape=pltpu.VMEM((tr, W), bf16),
        in_specs=[any_spec] * 3,
        out_specs=pl.BlockSpec(memory_space=pltpu.VMEM),
        scratch_shapes=[
            pltpu.SMEM(pattern.shape, jnp.int32),
            pltpu.VMEM((tr, ti), bf16),
            pltpu.VMEM((K, half), bf16),
            pltpu.VMEM((tr, K), bf16),
            pltpu.VMEM((tr, K), bf16),
            pltpu.VMEM((PIECES, K, W // PIECES), bf16),
            pltpu.VMEM((tr, W), jnp.float32),
            pltpu.SemaphoreType.REGULAR((3,)),
            dma((2 + PIECES,)),
            dma((A,)), dma((A,)), dma((B,)), dma((B,)),
            dma((B, A)), dma((B, A)), dma((B, A)), dma((B, A)),
            dma((C,)), dma((C,)), dma((C,)), dma((C,)),
            dma((C,)), dma((C,)), dma((C,)), dma((C,)),
            dma((A, PIECES)), dma((A, PIECES)),
            dma((B, PIECES)), dma((B, PIECES)),
            dma((B, A, PIECES)), dma((B, A, PIECES)),
            dma((B, A, PIECES)), dma((B, A, PIECES)),
        ],
        compiler_params=pltpu.CompilerParams(
            collective_id=0, has_side_effects=True, vmem_limit_bytes=56 * 1024 * 1024
        ),
    )(density, panel, pattern)


def solution(mesh):
    R, C, L = mesh.shape["row"], mesh.shape["col"], mesh.shape["layer"]
    in_specs = (P("row", "col"), P("row", "col"), P("row", "col"))
    out_specs = P("row", ("col", "layer"))
    return jax.shard_map(
        functools.partial(shards, R, C, L),
        mesh=mesh, in_specs=in_specs, out_specs=out_specs, check_vma=False,
    )
```

```python
import functools

import jax
import jax.numpy as jnp
from jax import lax
from jax.experimental import pallas as pl
from jax.experimental.pallas import tpu as pltpu
from jax.sharding import PartitionSpec as P

BS = 128
PIECES = 4
MESH = pl.DeviceIdType.MESH


def kernel(
    sizes, density_ref, panel_ref, pattern_hbm, out_ref,
    pattern_ref, tile, fcol, frow, grow, p, acc,
    go, load_sem, cx_s, cx_r, cy_s, cy_r, ex_s, ex_r, ey_s, ey_r, fr_s, fr_r, fs_s, fs_r, gr_s, gr_r, gs_s, gs_r,
    px_s, px_r, py_s, py_r, fx_s, fx_r, fy_s, fy_r,
):
    R, A, C = sizes
    B = R // A
    tr, ti = density_ref.shape
    half = ti // 2
    wq = p.shape[2]
    W = wq * PIECES
    r = lax.axis_index("row")
    c = lax.axis_index("col")
    l = lax.axis_index("layer")
    x = lax.rem(r, A)
    y = r // A
    sib = 1 - l

    def rem_copy(ref, ssem, rsem, dev):
        return pltpu.make_async_remote_copy(
            src_ref=ref, dst_ref=ref, send_sem=ssem, recv_sem=rsem,
            device_id=dev, device_id_type=MESH,
        )

    def x_peer(d):
        return y * A + lax.rem(x + d, A)

    def y_peer(d):
        return lax.rem(y + d, B) * A + x

    barrier = pltpu.get_barrier_semaphore()
    def greet(sem, peers):
        for peer in peers:
            pl.semaphore_signal(sem, inc=1, device_id=peer, device_id_type=MESH)

    row_peers = [{"row": x_peer(d)} for d in range(1, A)] + [{"row": y_peer(d)} for d in range(1, B)]
    col_peers = [{"col": lax.rem(c + d, C)} for d in range(1, C)]
    sibling = [{"layer": sib}]

    @pl.when(l == 0)
    def _():
        greet(barrier, row_peers + sibling)

    @pl.when(l == 1)
    def _():
        greet(barrier, col_peers + sibling)

    load_pattern = pltpu.make_async_copy(pattern_hbm, pattern_ref, load_sem.at[1])
    load_pattern.start()
    load_tile = pltpu.make_async_copy(density_ref, tile, load_sem.at[0])
    load_tile.start()
    load_panel = []
    for q in range(PIECES):
        at = pl.ds(pl.multiple_of(l * W + q * wq, wq), wq)
        load_panel.append(pltpu.make_async_copy(panel_ref.at[:, at], p.at[q, 0:tr, :], load_sem.at[2 + q]))
        load_panel[q].start()
    first, second = range(PIECES // 2), range(PIECES // 2, PIECES)

    def cols_of(col, layer, width=half, extra=0):
        at = col * ti + layer * half + extra
        row = at // tr
        dy, dx = lax.rem(y - row // A + B, B), lax.rem(x - lax.rem(row, A) + A, A)
        return pl.ds(pl.multiple_of((dy * A + dx) * tr + lax.rem(at, tr), width), width)

    def rows_of(slot):
        return slice(slot * tr, (slot + 1) * tr)

    def half_rows(slot, which):
        return fcol.at[slot * tr + which * (tr // 2):slot * tr + (which + 1) * (tr // 2), :]

    def piece(slot, q):
        return p.at[q, rows_of(slot), :]

    def x_source(d):
        return y * A + lax.rem(x - d + A, A)

    def y_source(d):
        return lax.rem(y - d + B, B) * A + x

    sends = []

    def prepare(ref, ssem, rsem, dev, src=None):
        copy = pltpu.make_async_remote_copy(
            src_ref=ref if src is None else src, dst_ref=ref, send_sem=ssem, recv_sem=rsem,
            device_id=dev, device_id_type=MESH,
        )
        sends.append(copy)
        return copy

    def send(*args):
        prepare(*args).start()

    def arrived(ref, ssem, rsem, dev):
        rem_copy(ref, ssem, rsem, dev).wait_recv()

    x_order = list(second) + list(first)
    y_order = list(first) + list(second)

    def own_piece(n):
        qx, qy = x_order[n], y_order[n]
        return [
            prepare(piece(d, qx), px_s.at[d, qx], px_r.at[d, qx], {"row": x_peer(d)}, piece(0, qx))
            for d in range(1, A)
        ] + [
            prepare(piece(d * A, qy), py_s.at[d, qy], py_r.at[d, qy], {"row": y_peer(d)}, piece(0, qy))
            for d in range(1, B)
        ]

    load_pattern.wait()
    load_tile.wait()
    for a in range(tr // BS):
        for b in range(ti // BS):
            keep = pattern_ref[a, b].astype(jnp.float32)
            block = tile[a * BS:(a + 1) * BS, b * BS:(b + 1) * BS].astype(jnp.float32) * keep
            frow[a * BS:(a + 1) * BS, cols_of(c, 0, BS, b * BS)] = block.astype(jnp.bfloat16)
    fcol[rows_of(0), :] = frow[:, cols_of(c, l)]

    own_rows = fcol.at[rows_of(0), :]
    over_col = [
        prepare(frow.at[:, cols_of(c, l)], fr_s.at[d], fr_r.at[d], {"col": lax.rem(c + d, C)})
        for d in range(1, C)
    ]
    over_row = [
        prepare(fcol.at[rows_of(d), :], cx_s.at[d], cx_r.at[d], {"row": x_peer(d)}, own_rows)
        for d in range(1, A)
    ] + [
        prepare(fcol.at[rows_of(d * A), :], cy_s.at[d], cy_r.at[d], {"row": y_peer(d)}, own_rows)
        for d in range(1, B)
    ]
    for n in range(2):
        over_row += own_piece(n)
    for copy in load_panel:
        copy.wait()

    @pl.when(l == 0)
    def _():
        pl.semaphore_wait(barrier, len(row_peers) + 1)
        greet(go.at[0], row_peers)
        for copy in over_row:
            copy.start()
        pl.semaphore_wait(go.at[0], len(row_peers))
        greet(go.at[2], sibling)
        pl.semaphore_wait(go.at[2], 1)
        for copy in over_col:
            copy.start()

    @pl.when(l == 1)
    def _():
        pl.semaphore_wait(barrier, len(col_peers) + 1)
        greet(go.at[1], col_peers)
        for copy in over_col:
            copy.start()
        pl.semaphore_wait(go.at[1], len(col_peers))
        greet(go.at[2], sibling)
        pl.semaphore_wait(go.at[2], 1)
        for copy in over_row:
            copy.start()

    for dy in range(1, B):
        arrived(fcol.at[rows_of(dy * A), :], cy_s.at[dy], cy_r.at[dy], {"row": y_source(dy)})
        for dx in range(1, A):
            send(half_rows(dy * A + dx, 0), ex_s.at[dy, dx], ex_r.at[dy, dx], {"row": x_peer(dx)},
                 half_rows(dy * A, 0))
    for dx in range(1, A):
        arrived(fcol.at[rows_of(dx), :], cx_s.at[dx], cx_r.at[dx], {"row": x_source(dx)})
        for dy in range(1, B):
            send(half_rows(dy * A + dx, 1), ey_s.at[dy, dx], ey_r.at[dy, dx], {"row": y_peer(dy)},
                 half_rows(dx, 1))

    for n in range(2, PIECES):
        for copy in own_piece(n):
            copy.start()

    forwards = []

    def forward(n):
        known = len(sends)
        qf, qs = first[n], second[n]
        for dy in range(1, B):
            arrived(piece(dy * A, qf), py_s.at[dy, qf], py_r.at[dy, qf], {"row": y_source(dy)})
            for dx in range(1, A):
                send(piece(dy * A + dx, qf), fx_s.at[dy, dx, qf], fx_r.at[dy, dx, qf],
                     {"row": x_peer(dx)}, piece(dy * A, qf))
        for dx in range(1, A):
            arrived(piece(dx, qs), px_s.at[dx, qs], px_r.at[dx, qs], {"row": x_source(dx)})
            for dy in range(1, B):
                send(piece(dy * A + dx, qs), fy_s.at[dy, dx, qs], fy_r.at[dy, dx, qs],
                     {"row": y_peer(dy)}, piece(dx, qs))
        forwards.extend(sends[known:])
        del sends[known:]

    forward(0)

    for d in range(1, C):
        from_c = lax.rem(c - d + C, C)
        ref = frow.at[:, cols_of(from_c, l)]
        arrived(ref, fr_s.at[d], fr_r.at[d], {"col": from_c})
        send(ref, fs_s.at[d], fs_r.at[d], {"layer": sib})
    for d in range(1, C):
        from_c = lax.rem(c - d + C, C)
        arrived(frow.at[:, cols_of(from_c, sib)], fs_s.at[d], fs_r.at[d], {"layer": sib})
    for dy in range(1, B):
        for dx in range(1, A):
            slot = dy * A + dx
            arrived(half_rows(slot, 0), ex_s.at[dy, dx], ex_r.at[dy, dx], {"row": x_source(dx)})
            arrived(half_rows(slot, 1), ey_s.at[dy, dx], ey_r.at[dy, dx], {"row": y_source(dy)})

    grow[:, cols_of(c, l)] = jnp.dot(
        frow[...], fcol[...], preferred_element_type=jnp.float32
    ).astype(jnp.bfloat16)
    for d in range(1, C):
        send(grow.at[:, cols_of(c, l)], gr_s.at[d], gr_r.at[d], {"col": lax.rem(c + d, C)})
    send(grow.at[:, cols_of(c, l)], gs_s.at[0], gs_r.at[0], {"layer": sib})

    def part(q):
        return slice(q * wq, (q + 1) * wq)

    def by(left, group, q):
        at = slice(group[0] * tr, group[1] * tr)
        return jnp.dot(left[:, at], p[q, at, :], preferred_element_type=jnp.float32)

    near = [(0, A)]
    for dy in range(1, B):
        if dy * A == near[-1][1]:
            near[-1] = (near[-1][0], dy * A + 1)
        else:
            near.append((dy * A, dy * A + 1))
    far = [(dy * A + 1, dy * A + A) for dy in range(1, B)]

    for n in range(1, len(first)):
        forward(n)

    for d in range(1, C):
        from_c = lax.rem(c - d + C, C)
        ref = grow.at[:, cols_of(from_c, l)]
        arrived(ref, gr_s.at[d], gr_r.at[d], {"col": from_c})
        send(ref, gs_s.at[d], gs_r.at[d], {"layer": sib})
    for qf, qs in zip(first, second):
        for dy in range(1, B):
            arrived(piece(dy * A, qs), py_s.at[dy, qs], py_r.at[dy, qs], {"row": y_source(dy)})
        for dx in range(1, A):
            arrived(piece(dx, qf), px_s.at[dx, qf], px_r.at[dx, qf], {"row": x_source(dx)})
        for q in (qf, qs):
            acc[:, part(q)] = 3.0 * sum(by(frow, group, q) for group in near)
    for d in range(C):
        from_c = lax.rem(c - d + C, C)
        arrived(grow.at[:, cols_of(from_c, sib)], gs_s.at[d], gs_r.at[d], {"layer": sib})
    for q in range(PIECES):
        acc[:, part(q)] -= 2.0 * sum(by(grow, group, q) for group in near)

    for copy in sends:
        copy.wait_send()
    for qf, qs in zip(first, second):
        for dy in range(1, B):
            for dx in range(1, A):
                slot = dy * A + dx
                arrived(piece(slot, qf), fx_s.at[dy, dx, qf], fx_r.at[dy, dx, qf], {"row": x_source(dx)})
                arrived(piece(slot, qs), fy_s.at[dy, dx, qs], fy_r.at[dy, dx, qs], {"row": y_source(dy)})
        for q in (qf, qs):
            total = acc[:, part(q)]
            for group in far:
                total = total + (3.0 * by(frow, group, q) - 2.0 * by(grow, group, q))
            out_ref[:, part(q)] = total.astype(jnp.bfloat16)

    for copy in forwards:
        copy.wait_send()


def shards(R, C, L, density, panel, pattern):
    A = 1
    while A * A < R:
        A *= 2
    B = R // A
    tr, ti = density.shape
    half = ti // L
    W = panel.shape[1] // L
    K = tr * R
    dma = pltpu.SemaphoreType.DMA
    any_spec = pl.BlockSpec(memory_space=pl.ANY)
    bf16 = jnp.bfloat16
    return pl.pallas_call(
        functools.partial(kernel, (R, A, C)),
        out_shape=pltpu.VMEM((tr, W), bf16),
        in_specs=[any_spec] * 3,
        out_specs=pl.BlockSpec(memory_space=pltpu.VMEM),
        scratch_shapes=[
            pltpu.SMEM(pattern.shape, jnp.int32),
            pltpu.VMEM((tr, ti), bf16),
            pltpu.VMEM((K, half), bf16),
            pltpu.VMEM((tr, K), bf16),
            pltpu.VMEM((tr, K), bf16),
            pltpu.VMEM((PIECES, K, W // PIECES), bf16),
            pltpu.VMEM((tr, W), jnp.float32),
            pltpu.SemaphoreType.REGULAR((3,)),
            dma((2 + PIECES,)),
            dma((A,)), dma((A,)), dma((B,)), dma((B,)),
            dma((B, A)), dma((B, A)), dma((B, A)), dma((B, A)),
            dma((C,)), dma((C,)), dma((C,)), dma((C,)),
            dma((C,)), dma((C,)), dma((C,)), dma((C,)),
            dma((A, PIECES)), dma((A, PIECES)),
            dma((B, PIECES)), dma((B, PIECES)),
            dma((B, A, PIECES)), dma((B, A, PIECES)),
            dma((B, A, PIECES)), dma((B, A, PIECES)),
        ],
        compiler_params=pltpu.CompilerParams(
            collective_id=0, has_side_effects=True, vmem_limit_bytes=56 * 1024 * 1024
        ),
    )(density, panel, pattern)


def solution(mesh):
    R, C, L = mesh.shape["row"], mesh.shape["col"], mesh.shape["layer"]
    in_specs = (P("row", "col"), P("row", "col"), P("row", "col"))
    out_specs = P("row", ("col", "layer"))
    return jax.shard_map(
        functools.partial(shards, R, C, L),
        mesh=mesh, in_specs=in_specs, out_specs=out_specs, check_vma=False,
    )
```

```python
import functools

import jax
import jax.numpy as jnp
from jax import lax
from jax.experimental import pallas as pl
from jax.experimental.pallas import tpu as pltpu
from jax.sharding import PartitionSpec as P

BS = 128
PIECES = 8
MESH = pl.DeviceIdType.MESH


def kernel(
    sizes, density_ref, panel_ref, pattern_hbm, out_ref,
    pattern_ref, tile, fcol, frow, grow, p, acc,
    go, load_sem, cx_s, cx_r, cy_s, cy_r, ex_s, ex_r, ey_s, ey_r, fr_s, fr_r, fs_s, fs_r, gr_s, gr_r, gs_s, gs_r,
    px_s, px_r, py_s, py_r, fx_s, fx_r, fy_s, fy_r,
):
    R, A, C = sizes
    B = R // A
    tr, ti = density_ref.shape
    half = ti // 2
    wq = p.shape[2]
    W = wq * PIECES
    r = lax.axis_index("row")
    c = lax.axis_index("col")
    l = lax.axis_index("layer")
    x = lax.rem(r, A)
    y = r // A
    sib = 1 - l

    def rem_copy(ref, ssem, rsem, dev):
        return pltpu.make_async_remote_copy(
            src_ref=ref, dst_ref=ref, send_sem=ssem, recv_sem=rsem,
            device_id=dev, device_id_type=MESH,
        )

    def x_peer(d):
        return y * A + lax.rem(x + d, A)

    def y_peer(d):
        return lax.rem(y + d, B) * A + x

    barrier = pltpu.get_barrier_semaphore()
    def greet(sem, peers):
        for peer in peers:
            pl.semaphore_signal(sem, inc=1, device_id=peer, device_id_type=MESH)

    row_peers = [{"row": x_peer(d)} for d in range(1, A)] + [{"row": y_peer(d)} for d in range(1, B)]
    col_peers = [{"col": lax.rem(c + d, C)} for d in range(1, C)]
    sibling = [{"layer": sib}]

    @pl.when(l == 0)
    def _():
        greet(barrier, row_peers + sibling)

    @pl.when(l == 1)
    def _():
        greet(barrier, col_peers + sibling)

    load_pattern = pltpu.make_async_copy(pattern_hbm, pattern_ref, load_sem.at[1])
    load_pattern.start()
    load_tile = pltpu.make_async_copy(density_ref, tile, load_sem.at[0])
    load_tile.start()
    load_panel = []
    for q in range(PIECES):
        at = pl.ds(pl.multiple_of(l * W + q * wq, wq), wq)
        load_panel.append(pltpu.make_async_copy(panel_ref.at[:, at], p.at[q, 0:tr, :], load_sem.at[2 + q]))
        load_panel[q].start()
    first, second = range(PIECES // 2), range(PIECES // 2, PIECES)

    def cols_of(col, layer, width=half, extra=0):
        at = col * ti + layer * half + extra
        row = at // tr
        dy, dx = lax.rem(y - row // A + B, B), lax.rem(x - lax.rem(row, A) + A, A)
        return pl.ds(pl.multiple_of((dy * A + dx) * tr + lax.rem(at, tr), width), width)

    def rows_of(slot):
        return slice(slot * tr, (slot + 1) * tr)

    def half_rows(slot, which):
        return fcol.at[slot * tr + which * (tr // 2):slot * tr + (which + 1) * (tr // 2), :]

    def piece(slot, q):
        return p.at[q, rows_of(slot), :]

    def x_source(d):
        return y * A + lax.rem(x - d + A, A)

    def y_source(d):
        return lax.rem(y - d + B, B) * A + x

    sends = []

    def prepare(ref, ssem, rsem, dev, src=None):
        copy = pltpu.make_async_remote_copy(
            src_ref=ref if src is None else src, dst_ref=ref, send_sem=ssem, recv_sem=rsem,
            device_id=dev, device_id_type=MESH,
        )
        sends.append(copy)
        return copy

    def send(*args):
        prepare(*args).start()

    def arrived(ref, ssem, rsem, dev):
        rem_copy(ref, ssem, rsem, dev).wait_recv()

    x_order = list(second) + list(first)
    y_order = list(first) + list(second)

    def own_piece(n):
        qx, qy = x_order[n], y_order[n]
        return [
            prepare(piece(d, qx), px_s.at[d, qx], px_r.at[d, qx], {"row": x_peer(d)}, piece(0, qx))
            for d in range(1, A)
        ] + [
            prepare(piece(d * A, qy), py_s.at[d, qy], py_r.at[d, qy], {"row": y_peer(d)}, piece(0, qy))
            for d in range(1, B)
        ]

    load_pattern.wait()
    load_tile.wait()
    for a in range(tr // BS):
        for b in range(ti // BS):
            keep = pattern_ref[a, b].astype(jnp.float32)
            block = tile[a * BS:(a + 1) * BS, b * BS:(b + 1) * BS].astype(jnp.float32) * keep
            frow[a * BS:(a + 1) * BS, cols_of(c, 0, BS, b * BS)] = block.astype(jnp.bfloat16)
    fcol[rows_of(0), :] = frow[:, cols_of(c, l)]

    own_rows = fcol.at[rows_of(0), :]
    over_col = [
        prepare(frow.at[:, cols_of(c, l)], fr_s.at[d], fr_r.at[d], {"col": lax.rem(c + d, C)})
        for d in range(1, C)
    ]
    over_row = [
        prepare(fcol.at[rows_of(d), :], cx_s.at[d], cx_r.at[d], {"row": x_peer(d)}, own_rows)
        for d in range(1, A)
    ] + [
        prepare(fcol.at[rows_of(d * A), :], cy_s.at[d], cy_r.at[d], {"row": y_peer(d)}, own_rows)
        for d in range(1, B)
    ]
    for n in range(PIECES // 2):
        over_row += own_piece(n)
    for copy in load_panel:
        copy.wait()

    @pl.when(l == 0)
    def _():
        pl.semaphore_wait(barrier, len(row_peers) + 1)
        greet(go.at[0], row_peers)
        for copy in over_row:
            copy.start()
        pl.semaphore_wait(go.at[0], len(row_peers))
        greet(go.at[2], sibling)
        pl.semaphore_wait(go.at[2], 1)
        for copy in over_col:
            copy.start()

    @pl.when(l == 1)
    def _():
        pl.semaphore_wait(barrier, len(col_peers) + 1)
        greet(go.at[1], col_peers)
        for copy in over_col:
            copy.start()
        pl.semaphore_wait(go.at[1], len(col_peers))
        greet(go.at[2], sibling)
        pl.semaphore_wait(go.at[2], 1)
        for copy in over_row:
            copy.start()

    for dy in range(1, B):
        arrived(fcol.at[rows_of(dy * A), :], cy_s.at[dy], cy_r.at[dy], {"row": y_source(dy)})
        for dx in range(1, A):
            send(half_rows(dy * A + dx, 0), ex_s.at[dy, dx], ex_r.at[dy, dx], {"row": x_peer(dx)},
                 half_rows(dy * A, 0))
    for dx in range(1, A):
        arrived(fcol.at[rows_of(dx), :], cx_s.at[dx], cx_r.at[dx], {"row": x_source(dx)})
        for dy in range(1, B):
            send(half_rows(dy * A + dx, 1), ey_s.at[dy, dx], ey_r.at[dy, dx], {"row": y_peer(dy)},
                 half_rows(dx, 1))

    for n in range(PIECES // 2, PIECES):
        for copy in own_piece(n):
            copy.start()

    forwards = []

    def forward(n):
        known = len(sends)
        qf, qs = first[n], second[n]
        for dy in range(1, B):
            arrived(piece(dy * A, qf), py_s.at[dy, qf], py_r.at[dy, qf], {"row": y_source(dy)})
            for dx in range(1, A):
                send(piece(dy * A + dx, qf), fx_s.at[dy, dx, qf], fx_r.at[dy, dx, qf],
                     {"row": x_peer(dx)}, piece(dy * A, qf))
        for dx in range(1, A):
            arrived(piece(dx, qs), px_s.at[dx, qs], px_r.at[dx, qs], {"row": x_source(dx)})
            for dy in range(1, B):
                send(piece(dy * A + dx, qs), fy_s.at[dy, dx, qs], fy_r.at[dy, dx, qs],
                     {"row": y_peer(dy)}, piece(dx, qs))
        forwards.extend(sends[known:])
        del sends[known:]

    for n in range(PIECES // 4):
        forward(n)

    for d in range(1, C):
        from_c = lax.rem(c - d + C, C)
        ref = frow.at[:, cols_of(from_c, l)]
        arrived(ref, fr_s.at[d], fr_r.at[d], {"col": from_c})
        send(ref, fs_s.at[d], fs_r.at[d], {"layer": sib})
    for d in range(1, C):
        from_c = lax.rem(c - d + C, C)
        arrived(frow.at[:, cols_of(from_c, sib)], fs_s.at[d], fs_r.at[d], {"layer": sib})
    for dy in range(1, B):
        for dx in range(1, A):
            slot = dy * A + dx
            arrived(half_rows(slot, 0), ex_s.at[dy, dx], ex_r.at[dy, dx], {"row": x_source(dx)})
            arrived(half_rows(slot, 1), ey_s.at[dy, dx], ey_r.at[dy, dx], {"row": y_source(dy)})

    grow[:, cols_of(c, l)] = jnp.dot(
        frow[...], fcol[...], preferred_element_type=jnp.float32
    ).astype(jnp.bfloat16)
    for d in range(1, C):
        send(grow.at[:, cols_of(c, l)], gr_s.at[d], gr_r.at[d], {"col": lax.rem(c + d, C)})
    send(grow.at[:, cols_of(c, l)], gs_s.at[0], gs_r.at[0], {"layer": sib})

    def part(q):
        return slice(q * wq, (q + 1) * wq)

    def by(left, group, q):
        at = slice(group[0] * tr, group[1] * tr)
        return jnp.dot(left[:, at], p[q, at, :], preferred_element_type=jnp.float32)

    near = [(0, A)]
    for dy in range(1, B):
        if dy * A == near[-1][1]:
            near[-1] = (near[-1][0], dy * A + 1)
        else:
            near.append((dy * A, dy * A + 1))
    far = [(dy * A + 1, dy * A + A) for dy in range(1, B)]

    for n in range(PIECES // 4, len(first)):
        forward(n)

    for d in range(1, C):
        from_c = lax.rem(c - d + C, C)
        ref = grow.at[:, cols_of(from_c, l)]
        arrived(ref, gr_s.at[d], gr_r.at[d], {"col": from_c})
        send(ref, gs_s.at[d], gs_r.at[d], {"layer": sib})
    for qf, qs in zip(first, second):
        for dy in range(1, B):
            arrived(piece(dy * A, qs), py_s.at[dy, qs], py_r.at[dy, qs], {"row": y_source(dy)})
        for dx in range(1, A):
            arrived(piece(dx, qf), px_s.at[dx, qf], px_r.at[dx, qf], {"row": x_source(dx)})
        for q in (qf, qs):
            acc[:, part(q)] = 3.0 * sum(by(frow, group, q) for group in near)
    for d in range(C):
        from_c = lax.rem(c - d + C, C)
        arrived(grow.at[:, cols_of(from_c, sib)], gs_s.at[d], gs_r.at[d], {"layer": sib})
    for q in range(PIECES):
        acc[:, part(q)] -= 2.0 * sum(by(grow, group, q) for group in near)

    for copy in sends:
        copy.wait_send()
    for qf, qs in zip(first, second):
        for dy in range(1, B):
            for dx in range(1, A):
                slot = dy * A + dx
                arrived(piece(slot, qf), fx_s.at[dy, dx, qf], fx_r.at[dy, dx, qf], {"row": x_source(dx)})
                arrived(piece(slot, qs), fy_s.at[dy, dx, qs], fy_r.at[dy, dx, qs], {"row": y_source(dy)})
        for q in (qf, qs):
            total = acc[:, part(q)]
            for group in far:
                total = total + (3.0 * by(frow, group, q) - 2.0 * by(grow, group, q))
            out_ref[:, part(q)] = total.astype(jnp.bfloat16)

    for copy in forwards:
        copy.wait_send()


def shards(R, C, L, density, panel, pattern):
    A = 1
    while A * A < R:
        A *= 2
    B = R // A
    tr, ti = density.shape
    half = ti // L
    W = panel.shape[1] // L
    K = tr * R
    dma = pltpu.SemaphoreType.DMA
    any_spec = pl.BlockSpec(memory_space=pl.ANY)
    bf16 = jnp.bfloat16
    return pl.pallas_call(
        functools.partial(kernel, (R, A, C)),
        out_shape=pltpu.VMEM((tr, W), bf16),
        in_specs=[any_spec] * 3,
        out_specs=pl.BlockSpec(memory_space=pltpu.VMEM),
        scratch_shapes=[
            pltpu.SMEM(pattern.shape, jnp.int32),
            pltpu.VMEM((tr, ti), bf16),
            pltpu.VMEM((K, half), bf16),
            pltpu.VMEM((tr, K), bf16),
            pltpu.VMEM((tr, K), bf16),
            pltpu.VMEM((PIECES, K, W // PIECES), bf16),
            pltpu.VMEM((tr, W), jnp.float32),
            pltpu.SemaphoreType.REGULAR((3,)),
            dma((2 + PIECES,)),
            dma((A,)), dma((A,)), dma((B,)), dma((B,)),
            dma((B, A)), dma((B, A)), dma((B, A)), dma((B, A)),
            dma((C,)), dma((C,)), dma((C,)), dma((C,)),
            dma((C,)), dma((C,)), dma((C,)), dma((C,)),
            dma((A, PIECES)), dma((A, PIECES)),
            dma((B, PIECES)), dma((B, PIECES)),
            dma((B, A, PIECES)), dma((B, A, PIECES)),
            dma((B, A, PIECES)), dma((B, A, PIECES)),
        ],
        compiler_params=pltpu.CompilerParams(
            collective_id=0, has_side_effects=True, vmem_limit_bytes=56 * 1024 * 1024
        ),
    )(density, panel, pattern)


def solution(mesh):
    R, C, L = mesh.shape["row"], mesh.shape["col"], mesh.shape["layer"]
    in_specs = (P("row", "col"), P("row", "col"), P("row", "col"))
    out_specs = P("row", ("col", "layer"))
    return jax.shard_map(
        functools.partial(shards, R, C, L),
        mesh=mesh, in_specs=in_specs, out_specs=out_specs, check_vma=False,
    )
```
